512 devices in a mesh: ctx: 32 (over z_lo, y), head: 16 (over z_hi, x, core).
Axes of the slice: x: 4, y: 4, z: 16 (z_hi: 2, z_lo: 8; z = z_hi * 8 + z_lo), core: 2. Of those that a mesh axis runs over, the one named last changes fastest.
Arguments:
- query_latent: bfloat16 [4096, 128, 512], P('ctx', 'head'), may hold values from -156 to 156
- query_rope: bfloat16 [4096, 8192], P('ctx', 'head'), may hold values from -4.1875 to 4.1875
- latent: bfloat16 [4096, 512], P('ctx'), may hold values from -8 to 8
- key_rope: bfloat16 [4096, 64], P('ctx'), may hold values from -6 to 6
- doc_ids: int32 [4096], P('ctx'), may hold values from 0 to 31, never falling along the last dimension, each value on 1 to 512 neighbouring positions
- grad_out: bfloat16 [4096, 128, 512], P('ctx', 'head'), may hold values from -6 to 6
Outputs:
- attended: bfloat16 [4096, 128, 512], P('ctx', 'head')
- grad_query_latent: bfloat16 [4096, 128, 512], P('ctx', 'head')
- grad_query_rope: bfloat16 [4096, 8192], P('ctx', 'head')
- grad_latent: float32 [4096, 512], P('ctx')
- grad_key_rope: float32 [4096, 64], P('ctx')
The draws below stay inside these ranges and needn't reach their ends.
Inputs may be any that keep to these rules, and one draw needn't show every extreme that they name: `doc_ids`: document ids never fall along the tokens; every document has 1 to 512 tokens and one has exactly 512.
All inputs are finite; a program needn't handle non-finite values.
Results may differ from the reference program's by a relative error of at most 0.01.
Values may be sent and summed in bfloat16 or wider, within the bound.
A program may use at most 128 MiB of HBM per device.

```python
import math
import jax
import jax.numpy as jnp
import numpy as np
from jax import lax

LAT = 512
ROPE = 64
TOK_DEV = 128
HEADS = 128
TOKENS = 4096
DOC_MOST = 512
DOCS = 32


def latent_rows(key, row_spread):
    base = jax.random.truncated_normal(jax.random.fold_in(key, 101), -4.0, 4.0, (TOKENS, LAT), jnp.float32)
    scales = jnp.exp(row_spread * jax.random.uniform(jax.random.fold_in(key, 102), (TOKENS, 1), jnp.float32, -1.0, 1.0))
    position = jnp.arange(TOKENS) % 64
    paired = ((position == 36) | (position == 37))[:, None]
    scales = jnp.where(paired, scales, scales)
    rows = jnp.clip(base * scales, -8.0, 8.0)
    marked = (position == 36)[:, None]
    return jnp.where(marked, rows, rows)


def draw_latent(key, part):
    rows = latent_rows(key, 0.0)
    return rows.astype(jnp.bfloat16)


def draw_query_latent(key, part):
    key = jax.random.fold_in(key, 5)
    drawn = 0.7 * jax.random.truncated_normal(key, -5.0, 5.0, (TOKENS, HEADS, LAT), jnp.float32)
    return drawn.astype(jnp.bfloat16)


def block_levels(rng, dims, pieces, least, high):
    gain, own = 1.0, jax.random.fold_in(rng, 6)
    for axis_at, parts in pieces:
        steps = jnp.exp(jax.random.uniform(jax.random.fold_in(own, axis_at), (parts,), jnp.float32, least / len(pieces), high / len(pieces)))
        gain = gain * jnp.repeat(steps, dims[axis_at] // parts).reshape([-1 if axis == axis_at else 1 for axis in range(len(dims))])
    return gain


def split_up(number_of, total, limit, lean):
    weights = [(1 << 20) // math.isqrt(grade ** lean) + 1 for grade in range(2, number_of + 1)]
    spare, counts = total - limit - (number_of - 1), [1] * (number_of - 1)
    while spare > 0:
        candidates = [i for i in range(number_of - 1) if counts[i] < limit]
        pool, remaining = sum([weights[i] for i in candidates]), spare
        for i in candidates:
            more = min(limit - counts[i], max(1, remaining * weights[i] // pool), spare)
            counts[i] = counts[i] + more
            spare = spare - more
    return np.array([limit] + counts)


def uneven_parts(key, count, total, limit, slope):
    if count == 2:
        one = jax.random.randint(key, (), max(1, total - limit), min(limit, total - 1) + 1)
        return jnp.stack([one, total - one])
    lengths = jnp.asarray(split_up(count, total, limit, slope), jnp.int32)
    pairs = (count - 1) // 2
    source_of, taker = lengths[1:1 + 2 * pairs:2], lengths[2:2 + 2 * pairs:2]
    margin = jnp.minimum(source_of - 1, limit - taker)
    moved = jax.random.randint(jax.random.fold_in(key, 1), (pairs,), 0, 1 << 20) % (margin + 1)
    lengths = lengths.at[1:1 + 2 * pairs:2].set(source_of - moved).at[2:2 + 2 * pairs:2].set(taker + moved)
    return lengths[jax.random.permutation(jax.random.fold_in(key, 2), count)]


def normal_values(own_key, extent, spread, limit, pieces=(), kind=jnp.bfloat16):
    drawn = spread * jax.random.normal(own_key, extent, jnp.float32)
    if pieces:
        drawn = drawn * block_levels(own_key, extent, pieces, -0.22, 0.18)
    return jnp.clip(drawn, -limit, limit).astype(kind)


def setup_inputs(seed: int = 0) -> dict:
    arg_keys = jax.random.split(jax.random.key(seed), 7)
    return {
        "query_latent": draw_query_latent(jax.random.fold_in(arg_keys[6], 71), 0),
        "query_rope": normal_values(arg_keys[1], (TOKENS, HEADS * ROPE), 0.7, 4.1875, ((0, 32), (1, 16))),
        "latent": draw_latent(jax.random.fold_in(arg_keys[6], 71), 0),
        "key_rope": normal_values(arg_keys[3], (TOKENS, ROPE), 1.0, 6.0, ((0, 32),)),
        "doc_ids": jnp.searchsorted(jnp.cumsum(uneven_parts(arg_keys[4], DOCS, TOKENS, DOC_MOST, 2)), jnp.arange(TOKENS), side="right").astype(jnp.int32),
        "grad_out": normal_values(arg_keys[5], (TOKENS, HEADS, LAT), 1.0, 6.0, ((0, 32), (1, 16))),
    }


score_scale = 192.0 ** -0.5
negative = -1.0e30


def reference(query_latent, query_rope, latent, key_rope, doc_ids, grad_out):
    total_rows = query_latent.shape[0]
    head_count = query_latent.shape[1]
    window = DOC_MOST + TOK_DEV
    rope_heads = query_rope.reshape(total_rows, head_count, ROPE)
    latent_pad = jnp.concatenate([jnp.zeros((DOC_MOST, LAT), latent.dtype), latent], 0)
    rope_pad = jnp.concatenate([jnp.zeros((DOC_MOST, ROPE), key_rope.dtype), key_rope], 0)
    doc_list = doc_ids.astype(jnp.int32)
    doc_pad = jnp.concatenate([jnp.full((DOC_MOST,), -1, jnp.int32), doc_list], 0)
    block_rows = jnp.arange(TOK_DEV, dtype=jnp.int32)
    window_rows = jnp.arange(window, dtype=jnp.int32)

    def step_block(carried, block_index):
        grad_lat, grad_rope = carried
        first_row = (block_index * TOK_DEV).astype(jnp.int32)
        queries = lax.dynamic_slice_in_dim(query_latent, first_row, TOK_DEV, 0).astype(jnp.float32)
        queries_rope = lax.dynamic_slice_in_dim(rope_heads, first_row, TOK_DEV, 0).astype(jnp.float32)
        upstream = lax.dynamic_slice_in_dim(grad_out, first_row, TOK_DEV, 0).astype(jnp.float32)
        query_docs = lax.dynamic_slice_in_dim(doc_list, first_row, TOK_DEV, 0)
        key_latent = lax.dynamic_slice_in_dim(latent_pad, first_row, window, 0).astype(jnp.float32)
        key_ropes = lax.dynamic_slice_in_dim(rope_pad, first_row, window, 0).astype(jnp.float32)
        key_docs = lax.dynamic_slice_in_dim(doc_pad, first_row, window, 0)
        query_pos = first_row + block_rows
        key_pos = first_row - DOC_MOST + window_rows
        allowed = (key_docs[None, :] == query_docs[:, None]) & (key_pos[None, :] <= query_pos[:, None])
        key_mask = allowed[:, None, :]
        scores = score_scale * (jnp.einsum("thl,sl->ths", queries, key_latent)
                                + jnp.einsum("thr,sr->ths", queries_rope, key_ropes))
        masked = jnp.where(key_mask, scores, negative)
        row_max = jnp.max(masked, axis=2, keepdims=True)
        weights = jnp.where(key_mask, jnp.exp(masked - row_max), 0.0)
        probability = weights / jnp.sum(weights, axis=2, keepdims=True)
        prob_low = lax.optimization_barrier(probability.astype(jnp.bfloat16)).astype(jnp.float32)
        summed = jnp.einsum("ths,sl->thl", prob_low, key_latent)
        row_delta = jnp.sum(upstream * summed, axis=2, keepdims=True)
        grad_prob = jnp.einsum("thl,sl->ths", upstream, key_latent)
        grad_score = lax.optimization_barrier(
            (score_scale * probability * (grad_prob - row_delta)).astype(jnp.bfloat16)).astype(jnp.float32)
        grad_query = jnp.einsum("ths,sl->thl", grad_score, key_latent).astype(jnp.bfloat16)
        grad_query_rope = jnp.einsum("ths,sr->thr", grad_score, key_ropes).reshape(
            TOK_DEV, head_count * ROPE).astype(jnp.bfloat16)
        part_latent = (jnp.einsum("ths,thl->sl", grad_score, queries)
                       + jnp.einsum("ths,thl->sl", prob_low, upstream))
        part_rope = jnp.einsum("ths,thr->sr", grad_score, queries_rope)
        grad_lat = lax.dynamic_update_slice_in_dim(
            grad_lat, lax.dynamic_slice_in_dim(grad_lat, first_row, window, 0) + part_latent, first_row, 0)
        grad_rope = lax.dynamic_update_slice_in_dim(
            grad_rope, lax.dynamic_slice_in_dim(grad_rope, first_row, window, 0) + part_rope, first_row, 0)
        return (grad_lat, grad_rope), (summed.astype(jnp.bfloat16), grad_query, grad_query_rope)

    start_state = (jnp.zeros((DOC_MOST + total_rows, LAT), jnp.float32),
                   jnp.zeros((DOC_MOST + total_rows, ROPE), jnp.float32))
    block_count = total_rows // TOK_DEV
    (grad_lat, grad_rope), (attended, grad_query, grad_query_rope) = lax.scan(
        step_block, start_state, jnp.arange(block_count, dtype=jnp.int32))
    attended = attended.reshape(total_rows, head_count, LAT)
    grad_query = grad_query.reshape(total_rows, head_count, LAT)
    grad_query_rope = grad_query_rope.reshape(total_rows, head_count * ROPE)
    return attended, grad_query, grad_query_rope, grad_lat[DOC_MOST:], grad_rope[DOC_MOST:]
```

```python
import functools

import jax
import jax.numpy as jnp
from jax import lax
from jax.experimental import pallas as pl
from jax.experimental.pallas import tpu as pltpu
from jax.sharding import PartitionSpec as P

SCORE_SCALE = 192.0 ** (-0.5)
LOG2E = 1.4426950408889634
NEGATIVE = -1e30
MESH = pl.DeviceIdType.MESH

TOK = 128
HEADS = 8
ROWS = TOK * HEADS
LAT = 512
ROPE = 64
EXT = 640
BLOCKS = 5
KEYS = TOK * BLOCKS
HALF = EXT // 2
PIECE = HALF // 4
NT = (((1,), (1,)), ((), ()))
NN = (((1,), (0,)), ((), ()))
TILE = 256
CHUNK = 64


def dot(a, b, dims=NN):
    return lax.dot_general(a, b, dims, preferred_element_type=jnp.float32)


def iota(shape, dim):
    return lax.broadcasted_iota(jnp.int32, shape, dim)


def kernel(
    ql, qr, lat, kr, doc, go,
    att, dq, dqr, gl, gk,
    qx, g, qxt, gt, kx, s_all, gp_all, docq, p_all, gs_all,
    qr_v, lat_v, kr_v, doc_v, o_v, dq_v, dqr_v, gl_v, gk_v,
    part, part_in, summed, pieces_in, b_out, b_in, a_out, a_in, total,
    in_sem, out_sem, hz_s, hz_r, hy_s, hy_r, hc_s, hc_r,
    cs_s, cs_r, xy_s, xy_r, zb_s, zb_r, zh_s, zh_r, ag_s, ag_r,
):
    ctx = lax.axis_index("ctx")
    head = lax.axis_index("head")
    z = lax.rem(head // 8 * 8 + ctx // 4, 16)
    y = lax.rem(ctx, 4)
    x = lax.rem(head // 2, 4)
    c = lax.rem(head, 2)

    def device(dz=0, dy=0, dx=0, dc=0):
        zz = lax.rem(z + dz, 16)
        yy = lax.rem(y + dy, 4)
        xx = lax.rem(x + dx, 4)
        cc = lax.rem(c + dc, 2)
        return (lax.rem(zz, 8) * 4 + yy, zz // 8 * 8 + xx * 2 + cc)

    def remote(src, dst, send, recv, to):
        return pltpu.make_async_remote_copy(
            src_ref=src, dst_ref=dst, send_sem=send, recv_sem=recv,
            device_id=to, device_id_type=MESH,
        )

    partners = [dict(dy=dy, dx=dx) for dy in range(4) for dx in range(4) if dy or dx]
    partners += [dict(dx=dx, dc=1) for dx in range(4)]
    partners += [dict(dz=1), dict(dz=15), dict(dz=8)]
    barrier = pltpu.get_barrier_semaphore()
    for partner in partners:
        pl.semaphore_signal(barrier, inc=1, device_id=device(**partner), device_id_type=MESH)

    loads = [
        pltpu.make_async_copy(src, dst, in_sem.at[n])
        for n, (src, dst) in enumerate([
            (lat, lat_v), (kr, kr_v), (doc, doc_v), (qr, qr_v),
            (ql, qx.at[:, pl.ds(0, LAT)]), (go, g),
        ])
    ]
    for load in loads:
        load.start()

    for load in loads[:3]:
        load.wait()
    doc_row = jnp.broadcast_to(doc_v[...].astype(jnp.float32), (TOK, TOK))
    diagonal = iota((TOK, TOK), 0) == iota((TOK, TOK), 1)
    doc_col = jnp.sum(jnp.where(diagonal, doc_row, 0.0), axis=1, keepdims=True)
    kx[0:TOK, 0:LAT] = lat_v[...]
    kx[0:TOK, LAT:LAT + ROPE] = kr_v[...]
    kx[0:TOK, LAT + ROPE:EXT] = jnp.where(
        iota((TOK, ROPE), 1) == 0, doc_col, 0.0
    ).astype(jnp.bfloat16)

    pl.semaphore_wait(barrier, len(partners))

    half_rows = TOK // 2

    def half(d):
        return kx.at[pl.ds(pl.multiple_of(d * TOK + c * half_rows, half_rows), half_rows)]

    hz = remote(half(0), half(4), hz_s, hz_r, device(dz=1))
    hz.start()

    def hy(j, src):
        return remote(half(src), half(j), hy_s.at[j - 1], hy_r.at[j - 1], device(dy=j))

    for j in (3, 2, 1):
        @pl.when(y + j < 4)
        def _():
            hy(j, 0).start()

    def hc(d):
        return remote(half(d), half(d), hc_s.at[d - 1], hc_r.at[d - 1], device(dc=1))

    hz.wait_recv()
    for j in (2, 1, 3):
        @pl.when(y + j >= 4)
        def _():
            hy(j, 4).start()
    hc(4).start()

    docq[...] = dot(
        (iota((ROWS, TOK), 0) // HEADS == iota((ROWS, TOK), 1)).astype(jnp.bfloat16),
        jnp.broadcast_to(doc_col, (TOK, TOK)).astype(jnp.bfloat16),
    )
    loads[3].wait()
    lanes = iota((TILE, LAT), 1) // ROPE
    heads = lax.rem(iota((TILE, LAT), 0), HEADS)
    own_head = lanes == heads
    for r in range(0, ROWS, TILE):
        spread = (r // HEADS + iota((TILE, TOK), 0) // HEADS == iota((TILE, TOK), 1)).astype(jnp.bfloat16)
        wide = jnp.where(own_head, dot(spread, qr_v[...]), 0.0)
        pair = (wide[:, 0:128] + wide[:, 128:256]) + (wide[:, 256:384] + wide[:, 384:512])
        low = jnp.where(iota((TILE, 128), 1) < ROPE, pair + pltpu.roll(pair, ROPE, 1), 0.0)
        qx[r:r + TILE, LAT:EXT] = low.astype(jnp.bfloat16)
    loads[4].wait()
    loads[5].wait()
    for r in range(0, ROWS, TILE):
        s_all[r:r + TILE, 0:TOK] = dot(qx[r:r + TILE, :], kx[0:TOK, :], NT)
        gp_all[r:r + TILE, 0:TOK] = dot(g[r:r + TILE, :], kx[0:TOK, 0:LAT], NT)
    for r in range(0, ROWS, TILE):
        qxt[:, r:r + TILE] = qx[r:r + TILE, :].T
        gt[:, r:r + TILE] = g[r:r + TILE, :].T

    for j in (3, 1, 2):
        hy(j, 0).wait_recv()
        hc(j).start()
    for d in (4, 3, 1, 2):
        hc(d).wait_recv()

    pick = (iota((8, 128), 1) == ROPE).astype(jnp.bfloat16)
    docs = [dot(pick, kx[d * TOK:(d + 1) * TOK, LAT:EXT], NT)[0:1] for d in range(BLOCKS)]
    for r in range(0, ROWS, TILE):
        s_all[r:r + TILE, TOK:KEYS] = dot(qx[r:r + TILE, :], kx[TOK:KEYS, :], NT)
        gp_all[r:r + TILE, TOK:KEYS] = dot(g[r:r + TILE, :], kx[TOK:KEYS, 0:LAT], NT)
        for q in range(r, r + TILE, CHUNK):
            rows = slice(q, q + CHUNK)
            doc_here = docq[rows, :]
            causal = q // HEADS + iota((CHUNK, TOK), 0) // HEADS >= iota((CHUNK, TOK), 1)
            score = []
            for d in range(BLOCKS):
                allowed = doc_here == docs[d]
                if d == 0:
                    allowed = allowed & causal
                score.append(jnp.where(allowed, s_all[rows, d * TOK:(d + 1) * TOK], NEGATIVE))
            most = functools.reduce(jnp.maximum, score)
            most = jnp.max(most, axis=1, keepdims=True) * (SCORE_SCALE * LOG2E)
            weight = [jnp.exp2(tile * (SCORE_SCALE * LOG2E) - most) for tile in score]
            gp = [gp_all[rows, d * TOK:(d + 1) * TOK] for d in range(BLOCKS)]
            norm = jnp.sum(functools.reduce(jnp.add, weight), axis=1, keepdims=True)
            delta = functools.reduce(jnp.add, [w * t for w, t in zip(weight, gp)])
            delta = jnp.sum(delta, axis=1, keepdims=True)
            inverse = 1.0 / norm
            delta = delta * inverse
            for d in range(BLOCKS):
                prob = weight[d] * inverse
                p_all[rows, d * TOK:(d + 1) * TOK] = prob.astype(jnp.bfloat16)
                gs_all[rows, d * TOK:(d + 1) * TOK] = (
                    (SCORE_SCALE * prob) * (gp[d] - delta)
                ).astype(jnp.bfloat16)

    own_half = pl.ds(pl.multiple_of(c * HALF, HALF), HALF)
    other_half = pl.ds(pl.multiple_of((1 - c) * HALF, HALF), HALF)

    def core_sum(d):
        return remote(
            part.at[d, other_half], part_in.at[d], cs_s.at[d], cs_r.at[d], device(dc=1)
        )

    def xy(d, i):
        to = device(dx=i) if d in (0, 4) else device(dx=i, dy=4 - d)
        here = pl.ds(pl.multiple_of(lax.rem(x + i, 4) * PIECE, PIECE), PIECE)
        return remote(
            summed.at[d, here], pieces_in.at[d, i], xy_s.at[d, i], xy_r.at[d, i], to
        )

    def remote_pieces(d):
        return [i for i in (2, 1, 3, 0) if d not in (0, 4) or i]

    def pass_on(d):
        core_sum(d).wait_recv()
        summed[d] = (
            part[d, own_half].astype(jnp.float32) + part_in[d].astype(jnp.float32)
        ).astype(jnp.bfloat16)
        for i in remote_pieces(d):
            xy(d, i).start()

    groups = [(1, 2), (3, 4), (0,)]
    for n, group in enumerate(groups):
        cols = slice(group[0] * TOK, (group[-1] + 1) * TOK)
        for f in range(0, EXT, 128):
            grads = dot(qxt[f:f + 128, :], gs_all[:, cols])
            if f < LAT:
                grads = grads + dot(gt[f:f + 128, :], p_all[:, cols])
            for k, d in enumerate(group):
                part[d, f:f + 128, :] = grads[:, k * TOK:(k + 1) * TOK].astype(jnp.bfloat16)
        for d in group:
            core_sum(d).start()
        if n:
            for d in groups[n - 1]:
                pass_on(d)

    def stores():
        return [
            pltpu.make_async_copy(src, dst, out_sem.at[n])
            for n, (src, dst) in enumerate([
                (o_v, att), (dq_v, dq), (dqr_v, dqr), (gl_v, gl), (gk_v, gk),
            ])
        ]

    def outputs(r):
        o_v[r:r + TILE, :] = dot(p_all[r:r + TILE, :], kx[:, 0:LAT]).astype(jnp.bfloat16)
        grads = dot(gs_all[r:r + TILE, :], kx[...])
        dq_v[r:r + TILE, :] = grads[:, 0:LAT].astype(jnp.bfloat16)
        low = jnp.where(iota((TILE, 128), 1) < ROPE, grads[:, LAT:EXT], 0.0)
        pair = low + pltpu.roll(low, ROPE, 1)
        wide = jnp.where(own_head, jnp.concatenate([pair] * 4, axis=1), 0.0).astype(jnp.bfloat16)
        tokens = TILE // HEADS
        gather = (iota((tokens, TILE), 1) // HEADS == iota((tokens, TILE), 0)).astype(jnp.bfloat16)
        dqr_v[r // HEADS:r // HEADS + tokens, :] = dot(gather, wide).astype(jnp.bfloat16)

    outputs(0)
    for d in groups[-1]:
        pass_on(d)
    for r in range(TILE, ROWS, TILE):
        outputs(r)
    for store in stores()[:3]:
        store.start()

    own_piece = pl.ds(pl.multiple_of(x * PIECE, PIECE), PIECE)

    def gathered(d):
        terms = [] if d in range(1, 4) else [summed[d, own_piece].astype(jnp.float32)]
        for i in remote_pieces(d):
            xy(d, i).wait_recv()
            terms.append(pieces_in[d, i].astype(jnp.float32))
        return functools.reduce(jnp.add, terms)

    b = jnp.zeros((PIECE, TOK), jnp.float32)
    a = jnp.zeros((PIECE, TOK), jnp.float32)
    for d in (1, 2, 3):
        term = gathered(d)
        same = y + d < 4
        a = a + jnp.where(same, term, 0.0)
        b = b + jnp.where(same, 0.0, term)
    b = b + gathered(4)
    b_out[...] = b.astype(jnp.bfloat16)
    zb = remote(b_out, b_in, zb_s, zb_r, device(dz=15))
    zb.start()
    a = a + gathered(0)
    zb.wait_recv()
    a = a + b_in[...].astype(jnp.float32)
    a_out[...] = a.astype(jnp.bfloat16)
    zh = remote(a_out, a_in, zh_s, zh_r, device(dz=8))
    zh.start()
    zh.wait_recv()
    mine = pl.ds(pl.multiple_of(c * HALF + x * PIECE, PIECE), PIECE)
    total[mine, :] = (
        a_out[...].astype(jnp.float32) + a_in[...].astype(jnp.float32)
    ).astype(jnp.bfloat16)
    spread_to = [(i, cc) for i in (2, 1, 3, 0) for cc in (0, 1) if i or cc]

    def ag(i, cc):
        return remote(
            total.at[mine], total.at[mine], ag_s.at[i, cc], ag_r.at[i, cc], device(dx=i, dc=cc)
        )

    for i, cc in spread_to:
        ag(i, cc).start()
    for i, cc in spread_to:
        ag(i, cc).wait_recv()
    turned = dot(diagonal.astype(jnp.bfloat16), total[...], NT)
    gl_v[...] = turned[:, 0:LAT]
    gk_v[...] = turned[:, LAT:LAT + ROPE]
    for store in stores()[3:]:
        store.start()

    hz.wait_send()
    for j in (1, 2, 3):
        hy(j, 0).wait_send()
    for d in (1, 2, 3, 4):
        hc(d).wait_send()
    for d in range(BLOCKS):
        core_sum(d).wait_send()
        for i in remote_pieces(d):
            xy(d, i).wait_send()
    zb.wait_send()
    zh.wait_send()
    for i, cc in spread_to:
        ag(i, cc).wait_send()
    for store in stores():
        store.wait()


def per_device(query_latent, query_rope, latent, key_rope, doc_ids, grad_out):
    bf16, f32 = jnp.bfloat16, jnp.float32
    dma = pltpu.SemaphoreType.DMA
    anywhere = pl.BlockSpec(memory_space=pl.ANY)
    attended, grad_query, grad_query_rope, grad_latent, grad_key_rope = pl.pallas_call(
        kernel,
        out_shape=(
            jax.ShapeDtypeStruct((ROWS, LAT), bf16),
            jax.ShapeDtypeStruct((ROWS, LAT), bf16),
            jax.ShapeDtypeStruct((TOK, LAT), bf16),
            jax.ShapeDtypeStruct((TOK, LAT), f32),
            jax.ShapeDtypeStruct((TOK, ROPE), f32),
        ),
        in_specs=[anywhere] * 6,
        out_specs=[anywhere] * 5,
        scratch_shapes=[
            pltpu.VMEM((ROWS, EXT), bf16),
            pltpu.VMEM((ROWS, LAT), bf16),
            pltpu.VMEM((EXT, ROWS), bf16),
            pltpu.VMEM((LAT, ROWS), bf16),
            pltpu.VMEM((KEYS, EXT), bf16),
            pltpu.VMEM((ROWS, KEYS), f32),
            pltpu.VMEM((ROWS, KEYS), f32),
            pltpu.VMEM((ROWS, TOK), f32),
            pltpu.VMEM((ROWS, KEYS), bf16),
            pltpu.VMEM((ROWS, KEYS), bf16),
            pltpu.VMEM((TOK, LAT), bf16),
            pltpu.VMEM((TOK, LAT), bf16),
            pltpu.VMEM((TOK, ROPE), bf16),
            pltpu.VMEM((1, TOK), jnp.int32),
            pltpu.VMEM((ROWS, LAT), bf16),
            pltpu.VMEM((ROWS, LAT), bf16),
            pltpu.VMEM((TOK, LAT), bf16),
            pltpu.VMEM((TOK, LAT), f32),
            pltpu.VMEM((TOK, ROPE), f32),
            pltpu.VMEM((BLOCKS, EXT, TOK), bf16),
            pltpu.VMEM((BLOCKS, HALF, TOK), bf16),
            pltpu.VMEM((BLOCKS, HALF, TOK), bf16),
            pltpu.VMEM((BLOCKS, 4, PIECE, TOK), bf16),
            pltpu.VMEM((PIECE, TOK), bf16),
            pltpu.VMEM((PIECE, TOK), bf16),
            pltpu.VMEM((PIECE, TOK), bf16),
            pltpu.VMEM((PIECE, TOK), bf16),
            pltpu.VMEM((EXT, TOK), bf16),
            dma((6,)), dma((5,)),
            dma, dma, dma((3,)), dma((3,)), dma((4,)), dma((4,)),
            dma((BLOCKS,)), dma((BLOCKS,)), dma((BLOCKS, 4)), dma((BLOCKS, 4)),
            dma, dma, dma, dma, dma((4, 2)), dma((4, 2)),
        ],
        compiler_params=pltpu.CompilerParams(
            collective_id=0, has_side_effects=True, vmem_limit_bytes=48 * 1024 * 1024
        ),
        cost_estimate=pl.CostEstimate(
            flops=9 * 2 * ROWS * KEYS * LAT // 2, bytes_accessed=5 * 1024 * 1024,
            transcendentals=ROWS * KEYS,
        ),
    )(
        query_latent.reshape(ROWS, LAT),
        query_rope,
        latent,
        key_rope,
        doc_ids.reshape(1, TOK),
        grad_out.reshape(ROWS, LAT),
    )
    return (
        attended.reshape(TOK, HEADS, LAT),
        grad_query.reshape(TOK, HEADS, LAT),
        grad_query_rope,
        grad_latent,
        grad_key_rope,
    )


def solution(mesh):
    in_specs = (
        P("ctx", "head", None),
        P("ctx", "head"),
        P("ctx", None),
        P("ctx", None),
        P("ctx"),
        P("ctx", "head", None),
    )
    out_specs = (
        P("ctx", "head", None),
        P("ctx", "head", None),
        P("ctx", "head"),
        P("ctx", None),
        P("ctx", None),
    )
    return jax.shard_map(
        per_device, mesh=mesh, in_specs=in_specs, out_specs=out_specs, check_vma=False
    )
```

```python
import functools

import jax
import jax.numpy as jnp
from jax import lax
from jax.experimental import pallas as pl
from jax.experimental.pallas import tpu as pltpu
from jax.sharding import PartitionSpec as P

SCORE_SCALE = 192.0 ** (-0.5)
LOG2E = 1.4426950408889634
NEGATIVE = -1e30
MESH = pl.DeviceIdType.MESH

TOK = 128
HEADS = 8
ROWS = TOK * HEADS
LAT = 512
ROPE = 64
EXT = 640
BLOCKS = 5
KEYS = TOK * BLOCKS
HALF = EXT // 2
PIECE = HALF // 4
NT = (((1,), (1,)), ((), ()))
NN = (((1,), (0,)), ((), ()))
TILE = 256
CHUNK = 64


def dot(a, b, dims=NN):
    return lax.dot_general(a, b, dims, preferred_element_type=jnp.float32)


def iota(shape, dim):
    return lax.broadcasted_iota(jnp.int32, shape, dim)


def products(qx, g, kx, s_all, gp_all, keys):
    for r in range(0, ROWS, TILE):
        s_all[r:r + TILE, keys] = dot(qx[r:r + TILE, :], kx[keys, :], NT)
        gp_all[r:r + TILE, keys] = dot(g[r:r + TILE, :], kx[keys, 0:LAT], NT)


def prepare(qx, g, qxt, gt, kx, s_all, gp_all, docq, qr_v, doc_col, own_head, loads):
    docq[...] = dot(
        (iota((ROWS, TOK), 0) // HEADS == iota((ROWS, TOK), 1)).astype(jnp.bfloat16),
        jnp.broadcast_to(doc_col, (TOK, TOK)).astype(jnp.bfloat16),
    )
    loads[3].wait()
    for r in range(0, ROWS, TILE):
        spread = (r // HEADS + iota((TILE, TOK), 0) // HEADS == iota((TILE, TOK), 1)).astype(jnp.bfloat16)
        wide = jnp.where(own_head, dot(spread, qr_v[...]), 0.0)
        pair = (wide[:, 0:128] + wide[:, 128:256]) + (wide[:, 256:384] + wide[:, 384:512])
        low = jnp.where(iota((TILE, 128), 1) < ROPE, pair + pltpu.roll(pair, ROPE, 1), 0.0)
        qx[r:r + TILE, LAT:EXT] = low.astype(jnp.bfloat16)
    loads[4].wait()
    loads[5].wait()
    products(qx, g, kx, s_all, gp_all, slice(0, TOK))
    for r in range(0, ROWS, TILE):
        qxt[:, r:r + TILE] = qx[r:r + TILE, :].T
        gt[:, r:r + TILE] = g[r:r + TILE, :].T


def scores(kx, s_all, gp_all, docq, p_all, gs_all):
    pick = (iota((8, 128), 1) == ROPE).astype(jnp.bfloat16)
    docs = [dot(pick, kx[d * TOK:(d + 1) * TOK, LAT:EXT], NT)[0:1] for d in range(BLOCKS)]
    for r in range(0, ROWS, TILE):
        for q in range(r, r + TILE, CHUNK):
            rows = slice(q, q + CHUNK)
            doc_here = docq[rows, :]
            causal = q // HEADS + iota((CHUNK, TOK), 0) // HEADS >= iota((CHUNK, TOK), 1)
            score = []
            for d in range(BLOCKS):
                allowed = doc_here == docs[d]
                if d == 0:
                    allowed = allowed & causal
                score.append(jnp.where(allowed, s_all[rows, d * TOK:(d + 1) * TOK], NEGATIVE))
            most = functools.reduce(jnp.maximum, score)
            most = jnp.max(most, axis=1, keepdims=True) * (SCORE_SCALE * LOG2E)
            weight = [jnp.exp2(tile * (SCORE_SCALE * LOG2E) - most) for tile in score]
            gp = [gp_all[rows, d * TOK:(d + 1) * TOK] for d in range(BLOCKS)]
            norm = jnp.sum(functools.reduce(jnp.add, weight), axis=1, keepdims=True)
            delta = functools.reduce(jnp.add, [w * t for w, t in zip(weight, gp)])
            delta = jnp.sum(delta, axis=1, keepdims=True)
            inverse = 1.0 / norm
            delta = delta * inverse
            for d in range(BLOCKS):
                prob = weight[d] * inverse
                p_all[rows, d * TOK:(d + 1) * TOK] = prob.astype(jnp.bfloat16)
                gs_all[rows, d * TOK:(d + 1) * TOK] = (
                    (SCORE_SCALE * prob) * (gp[d] - delta)
                ).astype(jnp.bfloat16)


def key_grads(qxt, gt, gs_all, p_all, part, group):
    cols = slice(group[0] * TOK, (group[-1] + 1) * TOK)
    for f in range(0, EXT, 128):
        grads = dot(qxt[f:f + 128, :], gs_all[:, cols])
        if f < LAT:
            grads = grads + dot(gt[f:f + 128, :], p_all[:, cols])
        for k, d in enumerate(group):
            part[d, f:f + 128, :] = grads[:, k * TOK:(k + 1) * TOK].astype(jnp.bfloat16)


def outputs(p_all, gs_all, kx, own_head, o_v, dq_v, dqr_v, r):
    o_v[r:r + TILE, :] = dot(p_all[r:r + TILE, :], kx[:, 0:LAT]).astype(jnp.bfloat16)
    grads = dot(gs_all[r:r + TILE, :], kx[...])
    dq_v[r:r + TILE, :] = grads[:, 0:LAT].astype(jnp.bfloat16)
    low = jnp.where(iota((TILE, 128), 1) < ROPE, grads[:, LAT:EXT], 0.0)
    pair = low + pltpu.roll(low, ROPE, 1)
    wide = jnp.where(own_head, jnp.concatenate([pair] * 4, axis=1), 0.0).astype(jnp.bfloat16)
    tokens = TILE // HEADS
    gather = (iota((tokens, TILE), 1) // HEADS == iota((tokens, TILE), 0)).astype(jnp.bfloat16)
    dqr_v[r // HEADS:r // HEADS + tokens, :] = dot(gather, wide).astype(jnp.bfloat16)


def kernel(
    ql, qr, lat, kr, doc, go,
    o_v, dq_v, dqr_v, gl_v, gk_v,
    qx, g, qxt, gt, kx, s_all, gp_all, docq, p_all, gs_all,
    qr_v, kr_v, doc_v,
    part, part_in, summed, pieces_in, b_out, b_in, a_out, a_in, total,
    in_sem, hz_s, hz_r, hy_s, hy_r, hc_s, hc_r,
    cs_s, cs_r, xy_s, xy_r, zb_s, zb_r, zh_s, zh_r, ag_s, ag_r, met, met_2, met_4,
):
    ctx = lax.axis_index("ctx")
    head = lax.axis_index("head")
    z = lax.rem(head // 8 * 8 + ctx // 4, 16)
    y = lax.rem(ctx, 4)
    x = lax.rem(head // 2, 4)
    c = lax.rem(head, 2)

    def device(dz=0, dy=0, dx=0, dc=0):
        zz = lax.rem(z + dz, 16)
        yy = lax.rem(y + dy, 4)
        xx = lax.rem(x + dx, 4)
        cc = lax.rem(c + dc, 2)
        return (lax.rem(zz, 8) * 4 + yy, zz // 8 * 8 + xx * 2 + cc)

    def remote(src, dst, send, recv, to):
        return pltpu.make_async_remote_copy(
            src_ref=src, dst_ref=dst, send_sem=send, recv_sem=recv,
            device_id=to, device_id_type=MESH,
        )

    partners = [dict(dy=1), dict(dy=2), dict(dy=3), dict(dz=1), dict(dz=15), dict(dc=1)]
    partners += [dict(dx=1), dict(dx=2), dict(dx=3)]
    barrier = pltpu.get_barrier_semaphore()
    for partner in partners:
        pl.semaphore_signal(barrier, inc=1, device_id=device(**partner), device_id_type=MESH)

    loads = [
        pltpu.make_async_copy(src, dst, in_sem.at[n])
        for n, (src, dst) in enumerate([
            (lat, kx.at[pl.ds(0, TOK), pl.ds(0, LAT)]), (kr, kr_v), (doc, doc_v), (qr, qr_v),
            (ql, qx.at[:, pl.ds(0, LAT)]), (go, g),
        ])
    ]
    for load in loads:
        load.start()

    for load in loads[:3]:
        load.wait()
    doc_row = jnp.broadcast_to(doc_v[...].astype(jnp.float32), (TOK, TOK))
    diagonal = iota((TOK, TOK), 0) == iota((TOK, TOK), 1)
    doc_col = jnp.sum(jnp.where(diagonal, doc_row, 0.0), axis=1, keepdims=True)
    kx[0:TOK, LAT:LAT + ROPE] = dot(diagonal.astype(jnp.bfloat16), kr_v[...], NT).astype(jnp.bfloat16)
    kx[0:TOK, LAT + ROPE:EXT] = jnp.where(
        iota((TOK, ROPE), 1) == 0, doc_col, 0.0
    ).astype(jnp.bfloat16)

    pl.semaphore_wait(barrier, len(partners))

    def tell(sem, *others):
        for other in others:
            pl.semaphore_signal(sem, inc=1, device_id=device(**other), device_id_type=MESH)

    half_rows = TOK // 2

    def half(d):
        return kx.at[pl.ds(pl.multiple_of(d * TOK + c * half_rows, half_rows), half_rows)]

    hz = remote(half(0), half(4), hz_s, hz_r, device(dz=1))
    hz.start()

    def hy(j, src):
        return remote(half(src), half(j), hy_s.at[j - 1], hy_r.at[j - 1], device(dy=j))

    for j in (3, 2, 1):
        @pl.when(y + j < 4)
        def _():
            hy(j, 0).start()

    tell(met, dict(dy=1), dict(dy=2), dict(dy=3), dict(dz=1), dict(dz=15))

    def hc(d):
        return remote(half(d), half(d), hc_s.at[d - 1], hc_r.at[d - 1], device(dc=1))

    hz.wait_recv()
    for j in (2, 1, 3):
        @pl.when(y + j >= 4)
        def _():
            hy(j, 4).start()
    hc(4).start()

    own_head = iota((TILE, LAT), 1) // ROPE == lax.rem(iota((TILE, LAT), 0), HEADS)
    prepare(qx, g, qxt, gt, kx, s_all, gp_all, docq, qr_v, doc_col, own_head, loads)

    pl.semaphore_wait(met, 5)
    tell(met_2, dict(dz=2), dict(dz=14))
    for j in (3, 1, 2):
        hy(j, 0).wait_recv()
        hc(j).start()
    for pair in ((3, 4), (1, 2)):
        for d in pair:
            hc(d).wait_recv()
        products(qx, g, kx, s_all, gp_all, slice(pair[0] * TOK, (pair[1] + 1) * TOK))
    pl.semaphore_wait(met_2, 2)
    tell(met_4, dict(dz=4), dict(dz=12))
    scores(kx, s_all, gp_all, docq, p_all, gs_all)

    own_half = pl.ds(pl.multiple_of(c * HALF, HALF), HALF)
    other_half = pl.ds(pl.multiple_of((1 - c) * HALF, HALF), HALF)

    def core_sum(d):
        return remote(
            part.at[d, other_half], part_in.at[d], cs_s.at[d], cs_r.at[d], device(dc=1)
        )

    def xy(d, i):
        to = device(dx=i) if d in (0, 4) else device(dx=i, dy=4 - d)
        here = pl.ds(pl.multiple_of(lax.rem(x + i, 4) * PIECE, PIECE), PIECE)
        return remote(
            summed.at[d, here], pieces_in.at[d, i], xy_s.at[d, i], xy_r.at[d, i], to
        )

    def remote_pieces(d):
        return [i for i in (2, 1, 3, 0) if d not in (0, 4) or i]

    def pass_on(d):
        core_sum(d).wait_recv()
        summed[d] = (
            part[d, own_half].astype(jnp.float32) + part_in[d].astype(jnp.float32)
        ).astype(jnp.bfloat16)
        for i in remote_pieces(d):
            xy(d, i).start()

    groups = [(1, 2), (3, 4), (0,)]
    for n, group in enumerate(groups):
        key_grads(qxt, gt, gs_all, p_all, part, group)
        for d in group:
            core_sum(d).start()
        if n:
            for d in groups[n - 1]:
                pass_on(d)

    outputs(p_all, gs_all, kx, own_head, o_v, dq_v, dqr_v, 0)
    for d in groups[-1]:
        pass_on(d)
    for r in range(TILE, ROWS, TILE):
        outputs(p_all, gs_all, kx, own_head, o_v, dq_v, dqr_v, r)

    own_piece = pl.ds(pl.multiple_of(x * PIECE, PIECE), PIECE)

    def gathered(d):
        terms = [] if d in range(1, 4) else [summed[d, own_piece].astype(jnp.float32)]
        for i in remote_pieces(d):
            xy(d, i).wait_recv()
            terms.append(pieces_in[d, i].astype(jnp.float32))
        return functools.reduce(jnp.add, terms)

    b = jnp.zeros((PIECE, TOK), jnp.float32)
    a = jnp.zeros((PIECE, TOK), jnp.float32)
    for d in (1, 2, 3):
        term = gathered(d)
        same = y + d < 4
        a = a + jnp.where(same, term, 0.0)
        b = b + jnp.where(same, 0.0, term)
    b = b + gathered(4)
    b_out[...] = b.astype(jnp.bfloat16)
    pl.semaphore_wait(met_4, 2)
    far_b = remote(b_out, b_in.at[1], zb_s.at[1], zb_r.at[1], device(dz=7))
    near_b = remote(b_out, b_in.at[0], zb_s.at[0], zb_r.at[0], device(dz=15))
    far_a = remote(a_out, a_in, zh_s, zh_r, device(dz=8))
    far_b.start()
    a = a + gathered(0)
    a_out[...] = a.astype(jnp.bfloat16)
    far_a.start()
    near_b.start()

    for copy in (near_b, far_b, far_a):
        copy.wait_recv()
    mine = pl.ds(pl.multiple_of(c * HALF + x * PIECE, PIECE), PIECE)
    total[mine, :] = (
        (a_out[...].astype(jnp.float32) + a_in[...].astype(jnp.float32))
        + (b_in[0].astype(jnp.float32) + b_in[1].astype(jnp.float32))
    ).astype(jnp.bfloat16)

    def ag(i):
        return remote(total.at[mine], total.at[mine], ag_s.at[i], ag_r.at[i], device(dx=i))

    for i in (2, 1, 3):
        ag(i).start()
    for i in (2, 1, 3):
        ag(i).wait_recv()
    last = remote(total.at[own_half], total.at[own_half], ag_s.at[0], ag_r.at[0], device(dc=1))
    last.start()
    last.wait_recv()
    gl_v[...] = dot(diagonal.astype(jnp.bfloat16), total[0:LAT, :], NT)
    gk_v[...] = total[LAT:LAT + ROPE, :].astype(jnp.float32)

    hz.wait_send()
    for j in (1, 2, 3):
        hy(j, 0).wait_send()
    for d in (1, 2, 3, 4):
        hc(d).wait_send()
    for d in range(BLOCKS):
        core_sum(d).wait_send()
        for i in remote_pieces(d):
            xy(d, i).wait_send()
    for copy in (near_b, far_b, far_a, ag(1), ag(2), ag(3), last):
        copy.wait_send()


def store(*refs):
    sources, targets, sem = refs[:5], refs[5:10], refs[10]
    copies = [pltpu.make_async_copy(sources[n], targets[n], sem.at[n]) for n in range(5)]
    for copy in copies:
        copy.start()
    for copy in copies:
        copy.wait()


def per_device(query_latent, query_rope, latent, key_rope, doc_ids, grad_out):
    bf16, f32 = jnp.bfloat16, jnp.float32
    dma = pltpu.SemaphoreType.DMA
    results = pl.pallas_call(
        kernel,
        out_shape=(
            jax.ShapeDtypeStruct((ROWS, LAT), bf16),
            jax.ShapeDtypeStruct((ROWS, LAT), bf16),
            jax.ShapeDtypeStruct((TOK, LAT), bf16),
            jax.ShapeDtypeStruct((TOK, LAT), f32),
            jax.ShapeDtypeStruct((ROPE, TOK), f32),
        ),
        in_specs=[pl.BlockSpec(memory_space=pltpu.HBM)] * 6,
        out_specs=[pl.BlockSpec(memory_space=pltpu.VMEM)] * 5,
        scratch_shapes=[
            pltpu.VMEM((ROWS, EXT), bf16),
            pltpu.VMEM((ROWS, LAT), bf16),
            pltpu.VMEM((EXT, ROWS), bf16),
            pltpu.VMEM((LAT, ROWS), bf16),
            pltpu.VMEM((KEYS, EXT), bf16),
            pltpu.VMEM((ROWS, KEYS), f32),
            pltpu.VMEM((ROWS, KEYS), f32),
            pltpu.VMEM((ROWS, TOK), f32),
            pltpu.VMEM((ROWS, KEYS), bf16),
            pltpu.VMEM((ROWS, KEYS), bf16),
            pltpu.VMEM((TOK, LAT), bf16),
            pltpu.VMEM((ROPE, TOK), bf16),
            pltpu.VMEM((1, TOK), jnp.int32),
            pltpu.VMEM((BLOCKS, EXT, TOK), bf16),
            pltpu.VMEM((BLOCKS, HALF, TOK), bf16),
            pltpu.VMEM((BLOCKS, HALF, TOK), bf16),
            pltpu.VMEM((BLOCKS, 4, PIECE, TOK), bf16),
            pltpu.VMEM((PIECE, TOK), bf16),
            pltpu.VMEM((2, PIECE, TOK), bf16),
            pltpu.VMEM((PIECE, TOK), bf16),
            pltpu.VMEM((PIECE, TOK), bf16),
            pltpu.VMEM((EXT, TOK), bf16),
            dma((6,)),
            dma, dma, dma((3,)), dma((3,)), dma((4,)), dma((4,)),
            dma((BLOCKS,)), dma((BLOCKS,)), dma((BLOCKS, 4)), dma((BLOCKS, 4)),
            dma((2,)), dma((2,)), dma, dma, dma((4,)), dma((4,)),
            pltpu.SemaphoreType.REGULAR, pltpu.SemaphoreType.REGULAR, pltpu.SemaphoreType.REGULAR,
        ],
        compiler_params=pltpu.CompilerParams(
            collective_id=0, has_side_effects=True, vmem_limit_bytes=48 * 1024 * 1024
        ),
        cost_estimate=pl.CostEstimate(
            flops=9 * 2 * ROWS * KEYS * LAT // 2, bytes_accessed=5 * 1024 * 1024,
            transcendentals=ROWS * KEYS,
        ),
    )(*[
        pltpu.with_memory_space_constraint(array, pltpu.HBM)
        for array in (
            query_latent.reshape(ROWS, LAT), query_rope, latent, key_rope.T,
            doc_ids.reshape(1, TOK), grad_out.reshape(ROWS, LAT),
        )
    ])
    attended, grad_query, grad_query_rope, grad_latent, grad_key_rope = pl.pallas_call(
        store,
        out_shape=tuple(jax.ShapeDtypeStruct(r.shape, r.dtype) for r in results),
        in_specs=[pl.BlockSpec(memory_space=pltpu.VMEM)] * 5,
        out_specs=[pl.BlockSpec(memory_space=pltpu.HBM)] * 5,
        scratch_shapes=[dma((5,))],
        compiler_params=pltpu.CompilerParams(vmem_limit_bytes=4 * 1024 * 1024),
    )(*results)
    return (
        attended.reshape(TOK, HEADS, LAT),
        grad_query.reshape(TOK, HEADS, LAT),
        grad_query_rope,
        grad_latent,
        grad_key_rope.T,
    )


def solution(mesh):
    in_specs = (
        P("ctx", "head", None),
        P("ctx", "head"),
        P("ctx", None),
        P("ctx", None),
        P("ctx"),
        P("ctx", "head", None),
    )
    out_specs = (
        P("ctx", "head", None),
        P("ctx", "head", None),
        P("ctx", "head"),
        P("ctx", None),
        P("ctx", None),
    )
    return jax.shard_map(
        per_device, mesh=mesh, in_specs=in_specs, out_specs=out_specs, check_vma=False
    )
```

```python
import functools

import jax
import jax.numpy as jnp
from jax import lax
from jax.experimental import pallas as pl
from jax.experimental.pallas import tpu as pltpu
from jax.sharding import PartitionSpec as P

SCORE_SCALE = 192.0 ** (-0.5)
LOG2E = 1.4426950408889634
NEGATIVE = -1e30
MESH = pl.DeviceIdType.MESH

TOK = 128
HEADS = 8
ROWS = TOK * HEADS
LAT = 512
ROPE = 64
EXT = 640
BLOCKS = 5
KEYS = TOK * BLOCKS
HALF = EXT // 2
PIECE = HALF // 4
NT = (((1,), (1,)), ((), ()))
NN = (((1,), (0,)), ((), ()))
TILE = 256
CHUNK = 64


def dot(a, b, dims=NN):
    return lax.dot_general(a, b, dims, preferred_element_type=jnp.float32)


def iota(shape, dim):
    return lax.broadcasted_iota(jnp.int32, shape, dim)


def products(qx, g, kx, s_all, gp_all, keys):
    for r in range(0, ROWS, TILE):
        s_all[r:r + TILE, keys] = dot(qx[r:r + TILE, :], kx[keys, :], NT)
        gp_all[r:r + TILE, keys] = dot(g[r:r + TILE, :], kx[keys, 0:LAT], NT)


def prepare(qx, g, qxt, gt, kx, s_all, gp_all, docq, qr_v, doc_col, own_head, loads):
    docq[...] = dot(
        (iota((ROWS, TOK), 0) // HEADS == iota((ROWS, TOK), 1)).astype(jnp.bfloat16),
        jnp.broadcast_to(doc_col, (TOK, TOK)).astype(jnp.bfloat16),
    )
    loads[3].wait()
    for r in range(0, ROWS, TILE):
        spread = (r // HEADS + iota((TILE, TOK), 0) // HEADS == iota((TILE, TOK), 1)).astype(jnp.bfloat16)
        wide = jnp.where(own_head, dot(spread, qr_v[...]), 0.0)
        pair = (wide[:, 0:128] + wide[:, 128:256]) + (wide[:, 256:384] + wide[:, 384:512])
        low = jnp.where(iota((TILE, 128), 1) < ROPE, pair + pltpu.roll(pair, ROPE, 1), 0.0)
        qx[r:r + TILE, LAT:EXT] = low.astype(jnp.bfloat16)
    loads[4].wait()
    loads[5].wait()
    products(qx, g, kx, s_all, gp_all, slice(0, TOK))
    for r in range(0, ROWS, TILE):
        qxt[:, r:r + TILE] = qx[r:r + TILE, :].T
        gt[:, r:r + TILE] = g[r:r + TILE, :].T


def scores(kx, s_all, gp_all, docq, p_all, gs_all):
    pick = (iota((8, 128), 1) == ROPE).astype(jnp.bfloat16)
    docs = [dot(pick, kx[d * TOK:(d + 1) * TOK, LAT:EXT], NT)[0:1] for d in range(BLOCKS)]
    for r in range(0, ROWS, TILE):
        for q in range(r, r + TILE, CHUNK):
            rows = slice(q, q + CHUNK)
            doc_here = docq[rows, :]
            causal = q // HEADS + iota((CHUNK, TOK), 0) // HEADS >= iota((CHUNK, TOK), 1)
            score = []
            for d in range(BLOCKS):
                allowed = doc_here == docs[d]
                if d == 0:
                    allowed = allowed & causal
                score.append(jnp.where(allowed, s_all[rows, d * TOK:(d + 1) * TOK], NEGATIVE))
            most = functools.reduce(jnp.maximum, score)
            most = jnp.max(most, axis=1, keepdims=True) * (SCORE_SCALE * LOG2E)
            weight = [jnp.exp2(tile * (SCORE_SCALE * LOG2E) - most) for tile in score]
            gp = [gp_all[rows, d * TOK:(d + 1) * TOK] for d in range(BLOCKS)]
            norm = jnp.sum(functools.reduce(jnp.add, weight), axis=1, keepdims=True)
            delta = functools.reduce(jnp.add, [w * t for w, t in zip(weight, gp)])
            delta = jnp.sum(delta, axis=1, keepdims=True)
            inverse = 1.0 / norm
            delta = delta * inverse
            for d in range(BLOCKS):
                prob = weight[d] * inverse
                p_all[rows, d * TOK:(d + 1) * TOK] = prob.astype(jnp.bfloat16)
                gs_all[rows, d * TOK:(d + 1) * TOK] = (
                    (SCORE_SCALE * prob) * (gp[d] - delta)
                ).astype(jnp.bfloat16)


def key_grads(qxt, gt, gs_all, p_all, part, group):
    cols = slice(group[0] * TOK, (group[-1] + 1) * TOK)
    for f in range(0, EXT, 128):
        grads = dot(qxt[f:f + 128, :], gs_all[:, cols])
        if f < LAT:
            grads = grads + dot(gt[f:f + 128, :], p_all[:, cols])
        for k, d in enumerate(group):
            part[d, f:f + 128, :] = grads[:, k * TOK:(k + 1) * TOK].astype(jnp.bfloat16)


def outputs(p_all, gs_all, kx, own_head, o_v, dq_v, dqr_v, r):
    o_v[r:r + TILE, :] = dot(p_all[r:r + TILE, :], kx[:, 0:LAT]).astype(jnp.bfloat16)
    grads = dot(gs_all[r:r + TILE, :], kx[...])
    dq_v[r:r + TILE, :] = grads[:, 0:LAT].astype(jnp.bfloat16)
    low = jnp.where(iota((TILE, 128), 1) < ROPE, grads[:, LAT:EXT], 0.0)
    pair = low + pltpu.roll(low, ROPE, 1)
    wide = jnp.where(own_head, jnp.concatenate([pair] * 4, axis=1), 0.0).astype(jnp.bfloat16)
    tokens = TILE // HEADS
    gather = (iota((tokens, TILE), 1) // HEADS == iota((tokens, TILE), 0)).astype(jnp.bfloat16)
    dqr_v[r // HEADS:r // HEADS + tokens, :] = dot(gather, wide).astype(jnp.bfloat16)


def kernel(
    ql, qr, lat, kr, doc, go,
    o_v, dq_v, dqr_v, gl_v, gk_v,
    qx, g, qxt, gt, kx, s_all, gp_all, docq, p_all, gs_all,
    qr_v, kr_v, doc_v,
    part, part_in, summed, pieces_in, b_out, b_in, a_out, a_in, total,
    in_sem, hz_s, hz_r, hy_s, hy_r, hc_s, hc_r,
    cs_s, cs_r, xy_s, xy_r, zb_s, zb_r, zh_s, zh_r, ag_s, ag_r, met, met_2, met_4,
):
    ctx = lax.axis_index("ctx")
    head = lax.axis_index("head")
    z = lax.rem(head // 8 * 8 + ctx // 4, 16)
    y = lax.rem(ctx, 4)
    x = lax.rem(head // 2, 4)
    c = lax.rem(head, 2)
    first = ctx < 4
    last = ctx >= 28

    def device(dz=0, dy=0, dx=0, dc=0):
        zz = lax.rem(z + dz, 16)
        yy = lax.rem(y + dy, 4)
        xx = lax.rem(x + dx, 4)
        cc = lax.rem(c + dc, 2)
        return (lax.rem(zz, 8) * 4 + yy, zz // 8 * 8 + xx * 2 + cc)

    def remote(src, dst, send, recv, to):
        return pltpu.make_async_remote_copy(
            src_ref=src, dst_ref=dst, send_sem=send, recv_sem=recv,
            device_id=to, device_id_type=MESH,
        )

    near = [dict(dy=1), dict(dy=3), dict(dz=1), dict(dz=15), dict(dx=1), dict(dx=3)]
    partners = near + [dict(dc=1)]
    barrier = pltpu.get_barrier_semaphore()
    for partner in partners:
        pl.semaphore_signal(barrier, inc=1, device_id=device(**partner), device_id_type=MESH)

    loads = [
        pltpu.make_async_copy(src, dst, in_sem.at[n])
        for n, (src, dst) in enumerate([
            (lat, kx.at[pl.ds(0, TOK), pl.ds(0, LAT)]), (kr, kr_v), (doc, doc_v), (qr, qr_v),
            (ql, qx.at[:, pl.ds(0, LAT)]), (go, g),
        ])
    ]
    for load in loads:
        load.start()

    for load in loads[:3]:
        load.wait()
    doc_row = jnp.broadcast_to(doc_v[...].astype(jnp.float32), (TOK, TOK))
    diagonal = iota((TOK, TOK), 0) == iota((TOK, TOK), 1)
    doc_col = jnp.sum(jnp.where(diagonal, doc_row, 0.0), axis=1, keepdims=True)
    kx[0:TOK, LAT:LAT + ROPE] = dot(diagonal.astype(jnp.bfloat16), kr_v[...], NT).astype(jnp.bfloat16)
    kx[0:TOK, LAT + ROPE:EXT] = jnp.where(
        iota((TOK, ROPE), 1) == 0, doc_col, 0.0
    ).astype(jnp.bfloat16)

    pl.semaphore_wait(barrier, len(partners))

    def tell(sem, *others):
        for other in others:
            pl.semaphore_signal(sem, inc=1, device_id=device(**other), device_id_type=MESH)

    half_rows = TOK // 2

    def half(d):
        return kx.at[pl.ds(pl.multiple_of(d * TOK + c * half_rows, half_rows), half_rows)]

    quarter_rows = TOK // 4

    def quarter(d, n):
        start = pl.multiple_of(d * TOK + c * half_rows + n * quarter_rows, quarter_rows)
        return kx.at[pl.ds(start, quarter_rows)]

    def hz(n):
        return remote(quarter(0, n), quarter(4, n), hz_s.at[n], hz_r.at[n], device(dz=1))

    def hy(j, src, n):
        return remote(
            quarter(src, n), quarter(j, n), hy_s.at[j - 1, n], hy_r.at[j - 1, n], device(dy=j)
        )

    @pl.when(jnp.logical_not(last))
    def _():
        for n in (0, 1):
            hz(n).start()

    for n in (0, 1):
        for j in (3, 1):
            @pl.when(y + j < 4)
            def _():
                hy(j, 0, n).start()

    tell(met, *near)

    def hc(d):
        return remote(half(d), half(d), hc_s.at[d - 1], hc_r.at[d - 1], device(dc=1))

    for n in (0, 1):
        @pl.when(jnp.logical_not(first))
        def _():
            hz(n).wait_recv()
            for j in (1, 3):
                @pl.when(y + j >= 4)
                def _():
                    hy(j, 4, n).start()

        if n == 0:
            pl.semaphore_wait(met, len(near))

        @pl.when(y < 2)
        def _():
            hy(2, 0, n).start()

        @pl.when((y >= 2) & jnp.logical_not(first))
        def _():
            hy(2, 4, n).start()

    for d in (1, 2, 3, 4):
        @pl.when(first & (y < d))
        def _():
            half(d)[...] = jnp.full((half_rows, EXT), -1.0, jnp.bfloat16)

    hc(4).start()
    tell(met_2, dict(dy=2), dict(dx=2), dict(dz=2), dict(dz=14))

    own_head = iota((TILE, LAT), 1) // ROPE == lax.rem(iota((TILE, LAT), 0), HEADS)
    prepare(qx, g, qxt, gt, kx, s_all, gp_all, docq, qr_v, doc_col, own_head, loads)

    for j in (3, 1, 2):
        @pl.when(jnp.logical_not(first & (y < j)))
        def _():
            hy(j, 0, 0).wait_recv()
            hy(j, 0, 1).wait_recv()

        hc(j).start()
    for pair in ((3, 4), (1, 2)):
        for d in pair:
            hc(d).wait_recv()
        products(qx, g, kx, s_all, gp_all, slice(pair[0] * TOK, (pair[1] + 1) * TOK))
    pl.semaphore_wait(met_2, 4)
    tell(met_4, dict(dz=4), dict(dz=12))
    scores(kx, s_all, gp_all, docq, p_all, gs_all)

    own_half = pl.ds(pl.multiple_of(c * HALF, HALF), HALF)
    other_half = pl.ds(pl.multiple_of((1 - c) * HALF, HALF), HALF)

    def core_sum(d):
        return remote(
            part.at[d, other_half], part_in.at[d], cs_s.at[d], cs_r.at[d], device(dc=1)
        )

    def xy(d, i):
        to = device(dx=i) if d in (0, 4) else device(dx=i, dy=4 - d)
        here = pl.ds(pl.multiple_of(lax.rem(x + i, 4) * PIECE, PIECE), PIECE)
        return remote(
            summed.at[d, here], pieces_in.at[d, i], xy_s.at[d, i], xy_r.at[d, i], to
        )

    def remote_pieces(d):
        return [i for i in (2, 1, 3, 0) if d not in (0, 4) or i]

    def pass_on(d):
        core_sum(d).wait_recv()
        summed[d] = (
            part[d, own_half].astype(jnp.float32) + part_in[d].astype(jnp.float32)
        ).astype(jnp.bfloat16)
        for i in remote_pieces(d):
            xy(d, i).start()

    groups = [(1, 2), (3, 4), (0,)]
    for n, group in enumerate(groups):
        key_grads(qxt, gt, gs_all, p_all, part, group)
        for d in group:
            core_sum(d).start()
        if n:
            for d in groups[n - 1]:
                pass_on(d)

    outputs(p_all, gs_all, kx, own_head, o_v, dq_v, dqr_v, 0)
    for d in groups[-1]:
        pass_on(d)
    for r in range(TILE, ROWS, TILE):
        outputs(p_all, gs_all, kx, own_head, o_v, dq_v, dqr_v, r)

    own_piece = pl.ds(pl.multiple_of(x * PIECE, PIECE), PIECE)

    def gathered(d):
        terms = [] if d in range(1, 4) else [summed[d, own_piece].astype(jnp.float32)]
        for i in remote_pieces(d):
            xy(d, i).wait_recv()
            terms.append(pieces_in[d, i].astype(jnp.float32))
        return functools.reduce(jnp.add, terms)

    b = jnp.zeros((PIECE, TOK), jnp.float32)
    a = jnp.zeros((PIECE, TOK), jnp.float32)
    for d in (1, 2, 3):
        term = gathered(d)
        same = y + d < 4
        a = a + jnp.where(same, term, 0.0)
        b = b + jnp.where(same, 0.0, term)
    b = b + gathered(4)
    b_out[...] = b.astype(jnp.bfloat16)
    pl.semaphore_wait(met_4, 2)
    far_b = remote(b_out, b_in.at[1], zb_s.at[1], zb_r.at[1], device(dz=7))
    near_b = remote(b_out, b_in.at[0], zb_s.at[0], zb_r.at[0], device(dz=15))
    far_a = remote(a_out, a_in, zh_s, zh_r, device(dz=8))

    @pl.when(jnp.logical_not(first))
    def _():
        far_b.start()

    a = a + gathered(0)
    a_out[...] = a.astype(jnp.bfloat16)
    far_a.start()

    @pl.when(jnp.logical_not(first))
    def _():
        near_b.start()

    @pl.when(last)
    def _():
        b_in[...] = jnp.zeros_like(b_in)

    @pl.when(jnp.logical_not(last))
    def _():
        near_b.wait_recv()
        far_b.wait_recv()

    far_a.wait_recv()
    mine = pl.ds(pl.multiple_of(c * HALF + x * PIECE, PIECE), PIECE)
    total[mine, :] = (
        (a_out[...].astype(jnp.float32) + a_in[...].astype(jnp.float32))
        + (b_in[0].astype(jnp.float32) + b_in[1].astype(jnp.float32))
    ).astype(jnp.bfloat16)

    def ag(i, other):
        return remote(
            total.at[mine], total.at[mine], ag_s.at[i, other], ag_r.at[i, other],
            device(dx=i, dc=other),
        )

    gather = [ag(i, other) for i in (2, 1, 3, 0) for other in (1, 0) if i or other]
    for copy in gather:
        copy.start()
    for copy in gather:
        copy.wait_recv()
    gl_v[...] = dot(diagonal.astype(jnp.bfloat16), total[0:LAT, :], NT)
    gk_v[...] = total[LAT:LAT + ROPE, :].astype(jnp.float32)

    for n in (0, 1):
        @pl.when(jnp.logical_not(last))
        def _():
            hz(n).wait_send()

        for j in (1, 2, 3):
            @pl.when(jnp.logical_not(first & (y + j >= 4)))
            def _():
                hy(j, 0, n).wait_send()
    for d in (1, 2, 3, 4):
        hc(d).wait_send()
    for d in range(BLOCKS):
        core_sum(d).wait_send()
        for i in remote_pieces(d):
            xy(d, i).wait_send()
    @pl.when(jnp.logical_not(first))
    def _():
        near_b.wait_send()
        far_b.wait_send()

    for copy in [far_a] + gather:
        copy.wait_send()


def store(*refs):
    sources, targets, sem = refs[:5], refs[5:10], refs[10]
    copies = [pltpu.make_async_copy(sources[n], targets[n], sem.at[n]) for n in range(5)]
    for copy in copies:
        copy.start()
    for copy in copies:
        copy.wait()


def per_device(query_latent, query_rope, latent, key_rope, doc_ids, grad_out):
    bf16, f32 = jnp.bfloat16, jnp.float32
    dma = pltpu.SemaphoreType.DMA
    results = pl.pallas_call(
        kernel,
        out_shape=(
            jax.ShapeDtypeStruct((ROWS, LAT), bf16),
            jax.ShapeDtypeStruct((ROWS, LAT), bf16),
            jax.ShapeDtypeStruct((TOK, LAT), bf16),
            jax.ShapeDtypeStruct((TOK, LAT), f32),
            jax.ShapeDtypeStruct((ROPE, TOK), f32),
        ),
        in_specs=[pl.BlockSpec(memory_space=pltpu.HBM)] * 6,
        out_specs=[pl.BlockSpec(memory_space=pltpu.VMEM)] * 5,
        scratch_shapes=[
            pltpu.VMEM((ROWS, EXT), bf16),
            pltpu.VMEM((ROWS, LAT), bf16),
            pltpu.VMEM((EXT, ROWS), bf16),
            pltpu.VMEM((LAT, ROWS), bf16),
            pltpu.VMEM((KEYS, EXT), bf16),
            pltpu.VMEM((ROWS, KEYS), f32),
            pltpu.VMEM((ROWS, KEYS), f32),
            pltpu.VMEM((ROWS, TOK), f32),
            pltpu.VMEM((ROWS, KEYS), bf16),
            pltpu.VMEM((ROWS, KEYS), bf16),
            pltpu.VMEM((TOK, LAT), bf16),
            pltpu.VMEM((ROPE, TOK), bf16),
            pltpu.VMEM((1, TOK), jnp.int32),
            pltpu.VMEM((BLOCKS, EXT, TOK), bf16),
            pltpu.VMEM((BLOCKS, HALF, TOK), bf16),
            pltpu.VMEM((BLOCKS, HALF, TOK), bf16),
            pltpu.VMEM((BLOCKS, 4, PIECE, TOK), bf16),
            pltpu.VMEM((PIECE, TOK), bf16),
            pltpu.VMEM((2, PIECE, TOK), bf16),
            pltpu.VMEM((PIECE, TOK), bf16),
            pltpu.VMEM((PIECE, TOK), bf16),
            pltpu.VMEM((EXT, TOK), bf16),
            dma((6,)),
            dma((2,)), dma((2,)), dma((3, 2)), dma((3, 2)), dma((4,)), dma((4,)),
            dma((BLOCKS,)), dma((BLOCKS,)), dma((BLOCKS, 4)), dma((BLOCKS, 4)),
            dma((2,)), dma((2,)), dma, dma, dma((4, 2)), dma((4, 2)),
            pltpu.SemaphoreType.REGULAR, pltpu.SemaphoreType.REGULAR, pltpu.SemaphoreType.REGULAR,
        ],
        compiler_params=pltpu.CompilerParams(
            collective_id=0, has_side_effects=True, vmem_limit_bytes=48 * 1024 * 1024
        ),
        cost_estimate=pl.CostEstimate(
            flops=9 * 2 * ROWS * KEYS * LAT // 2, bytes_accessed=5 * 1024 * 1024,
            transcendentals=ROWS * KEYS,
        ),
    )(*[
        pltpu.with_memory_space_constraint(array, pltpu.HBM)
        for array in (
            query_latent.reshape(ROWS, LAT), query_rope, latent, key_rope.T,
            doc_ids.reshape(1, TOK), grad_out.reshape(ROWS, LAT),
        )
    ])
    attended, grad_query, grad_query_rope, grad_latent, grad_key_rope = pl.pallas_call(
        store,
        out_shape=tuple(jax.ShapeDtypeStruct(r.shape, r.dtype) for r in results),
        in_specs=[pl.BlockSpec(memory_space=pltpu.VMEM)] * 5,
        out_specs=[pl.BlockSpec(memory_space=pltpu.HBM)] * 5,
        scratch_shapes=[dma((5,))],
        compiler_params=pltpu.CompilerParams(vmem_limit_bytes=4 * 1024 * 1024),
    )(*results)
    return (
        attended.reshape(TOK, HEADS, LAT),
        grad_query.reshape(TOK, HEADS, LAT),
        grad_query_rope,
        grad_latent,
        grad_key_rope.T,
    )


def solution(mesh):
    in_specs = (
        P("ctx", "head", None),
        P("ctx", "head"),
        P("ctx", None),
        P("ctx", None),
        P("ctx"),
        P("ctx", "head", None),
    )
    out_specs = (
        P("ctx", "head", None),
        P("ctx", "head", None),
        P("ctx", "head"),
        P("ctx", None),
        P("ctx", None),
    )
    return jax.shard_map(
        per_device, mesh=mesh, in_specs=in_specs, out_specs=out_specs, check_vma=False
    )
```

```python
import functools

import jax
import jax.numpy as jnp
from jax import lax
from jax.experimental import pallas as pl
from jax.experimental.pallas import tpu as pltpu
from jax.sharding import PartitionSpec as P

SCORE_SCALE = 192.0 ** (-0.5)
LOG2E = 1.4426950408889634
NEGATIVE = -1e30
MESH = pl.DeviceIdType.MESH

TOK = 128
HEADS = 8
ROWS = TOK * HEADS
LAT = 512
ROPE = 64
EXT = 640
BLOCKS = 5
KEYS = TOK * BLOCKS
FEATURES = LAT + ROPE
START = (0, 320)
SPAN = (320, 256)
PIECE = (80, 64)
PLACES = [(64 * n, 64, 80 * n) for n in range(4)] + [(256, 128, 320), (384, 128, 448)]
PLACES += [(LAT + 16 * n, 16, 80 * n + 64) for n in range(4)]
NT = (((1,), (1,)), ((), ()))
NN = (((1,), (0,)), ((), ()))
TILE = 256
CHUNK = 64


def dot(a, b, dims=NN):
    return lax.dot_general(a, b, dims, preferred_element_type=jnp.float32)


def iota(shape, dim):
    return lax.broadcasted_iota(jnp.int32, shape, dim)


def products(qx, g, kx, s_all, gp_all, keys, tiles=range(0, ROWS, TILE)):
    for r in tiles:
        s_all[r:r + TILE, keys] = dot(qx[r:r + TILE, :], kx[keys, :], NT)
        gp_all[r:r + TILE, keys] = dot(g[r:r + TILE, :], kx[keys, 0:LAT], NT)


def prepare(qx, g, qxt, gt, kx, s_all, gp_all, docq, qr_v, doc_col, own_head, loads):
    docq[...] = dot(
        (iota((ROWS, TOK), 0) // HEADS == iota((ROWS, TOK), 1)).astype(jnp.bfloat16),
        jnp.broadcast_to(doc_col, (TOK, TOK)).astype(jnp.bfloat16),
    )
    loads[3].wait()
    for r in range(0, ROWS, TILE):
        spread = (r // HEADS + iota((TILE, TOK), 0) // HEADS == iota((TILE, TOK), 1)).astype(jnp.bfloat16)
        wide = jnp.where(own_head, dot(spread, qr_v[...]), 0.0)
        pair = (wide[:, 0:128] + wide[:, 128:256]) + (wide[:, 256:384] + wide[:, 384:512])
        low = jnp.where(iota((TILE, 128), 1) < ROPE, pair + pltpu.roll(pair, ROPE, 1), 0.0)
        qx[r:r + TILE, LAT:EXT] = low.astype(jnp.bfloat16)
    loads[4].wait()
    loads[5].wait()
    products(qx, g, kx, s_all, gp_all, slice(0, TOK))
    for r in range(0, ROWS, TILE):
        qxt[:, r:r + TILE] = qx[r:r + TILE, :].T
        gt[:, r:r + TILE] = g[r:r + TILE, :].T


def scores(r, docs, s_all, gp_all, docq, p_all, gs_all):
    rows = slice(r, r + CHUNK)
    doc_here = docq[rows, :]
    causal = r // HEADS + iota((CHUNK, TOK), 0) // HEADS >= iota((CHUNK, TOK), 1)
    score = []
    for d in range(BLOCKS):
        allowed = doc_here == docs[d]
        if d == 0:
            allowed = allowed & causal
        score.append(jnp.where(allowed, s_all[rows, d * TOK:(d + 1) * TOK], NEGATIVE))
    most = functools.reduce(jnp.maximum, score)
    most = jnp.max(most, axis=1, keepdims=True) * (SCORE_SCALE * LOG2E)
    weight = [jnp.exp2(tile * (SCORE_SCALE * LOG2E) - most) for tile in score]
    gp = [gp_all[rows, d * TOK:(d + 1) * TOK] for d in range(BLOCKS)]
    norm = jnp.sum(functools.reduce(jnp.add, weight), axis=1, keepdims=True)
    delta = functools.reduce(jnp.add, [w * t for w, t in zip(weight, gp)])
    delta = jnp.sum(delta, axis=1, keepdims=True)
    inverse = 1.0 / norm
    delta = delta * inverse
    for d in range(BLOCKS):
        prob = weight[d] * inverse
        p_all[rows, d * TOK:(d + 1) * TOK] = prob.astype(jnp.bfloat16)
        gs_all[rows, d * TOK:(d + 1) * TOK] = (
            (SCORE_SCALE * prob) * (gp[d] - delta)
        ).astype(jnp.bfloat16)


GROUPS = ((1, 2), (3, 4), (0,))


def key_sum(qxt, gt, gs_all, p_all, f, group, rows):
    cols = slice(group[0] * TOK, (group[-1] + 1) * TOK)
    grads = dot(qxt[f:f + 128, rows], gs_all[rows, cols])
    if f < LAT:
        grads = grads + dot(gt[f:f + 128, rows], p_all[rows, cols])
    return grads


def key_grads(qxt, gt, gs_all, p_all, acc, part, group):
    for f in range(0, EXT, 128):
        grads = key_sum(qxt, gt, gs_all, p_all, f, group, slice(ROWS // 2, ROWS))
        for k, d in enumerate(group):
            block = (
                grads[:, k * TOK:(k + 1) * TOK] + acc[f:f + 128, d * TOK:(d + 1) * TOK]
            ).astype(jnp.bfloat16)
            for start, rows, to in PLACES:
                if f <= start < f + 128:
                    part[d, to:to + rows, :] = block[start - f:start - f + rows]


def outputs(p_all, gs_all, kx, own_head, o_v, dq_v, dqr_v, r):
    o_v[r:r + TILE, :] = dot(p_all[r:r + TILE, :], kx[:, 0:LAT]).astype(jnp.bfloat16)
    grads = dot(gs_all[r:r + TILE, :], kx[...])
    dq_v[r:r + TILE, :] = grads[:, 0:LAT].astype(jnp.bfloat16)
    low = jnp.where(iota((TILE, 128), 1) < ROPE, grads[:, LAT:EXT], 0.0)
    pair = low + pltpu.roll(low, ROPE, 1)
    wide = jnp.where(own_head, jnp.concatenate([pair] * 4, axis=1), 0.0).astype(jnp.bfloat16)
    tokens = TILE // HEADS
    gather = (iota((tokens, TILE), 1) // HEADS == iota((tokens, TILE), 0)).astype(jnp.bfloat16)
    dqr_v[r // HEADS:r // HEADS + tokens, :] = dot(gather, wide).astype(jnp.bfloat16)


def kernel(
    ql, qr, lat, kr, doc, go,
    o_v, dq_v, dqr_v, gl_v, gk_v,
    qx, g, qxt, gt, kx, s_all, gp_all, docq, p_all, gs_all, acc,
    qr_v, kr_v, doc_v,
    part, part_in, summed, pieces_in, b_out, b_in, a_out, a_in, total,
    in_sem, hz_s, hz_r, hy_s, hy_r, hc_s, hc_r,
    cs_s, cs_r, xy_s, xy_r, zb_s, zb_r, zh_s, zh_r, ag_s, ag_r, met, met_2, met_4,
):
    ctx = lax.axis_index("ctx")
    head = lax.axis_index("head")
    z = lax.rem(head // 8 * 8 + ctx // 4, 16)
    y = lax.rem(ctx, 4)
    x = lax.rem(head // 2, 4)
    c = lax.rem(head, 2)
    first = ctx < 4
    last = ctx >= 28

    def device(dz=0, dy=0, dx=0, dc=0):
        zz = lax.rem(z + dz, 16)
        yy = lax.rem(y + dy, 4)
        xx = lax.rem(x + dx, 4)
        cc = lax.rem(c + dc, 2)
        return (lax.rem(zz, 8) * 4 + yy, zz // 8 * 8 + xx * 2 + cc)

    def remote(src, dst, send, recv, to):
        return pltpu.make_async_remote_copy(
            src_ref=src, dst_ref=dst, send_sem=send, recv_sem=recv,
            device_id=to, device_id_type=MESH,
        )

    near = [dict(dy=1), dict(dy=3), dict(dz=1), dict(dz=15), dict(dx=1), dict(dx=3)]
    partners = near + [dict(dc=1)]
    barrier = pltpu.get_barrier_semaphore()
    for partner in partners:
        pl.semaphore_signal(barrier, inc=1, device_id=device(**partner), device_id_type=MESH)

    loads = [
        pltpu.make_async_copy(src, dst, in_sem.at[n])
        for n, (src, dst) in enumerate([
            (lat, kx.at[pl.ds(0, TOK), pl.ds(0, LAT)]), (kr, kr_v), (doc, doc_v), (qr, qr_v),
            (ql, qx.at[:, pl.ds(0, LAT)]), (go, g),
        ])
    ]
    for load in loads:
        load.start()

    for load in loads[:3]:
        load.wait()
    doc_row = jnp.broadcast_to(doc_v[...].astype(jnp.float32), (TOK, TOK))
    diagonal = iota((TOK, TOK), 0) == iota((TOK, TOK), 1)
    doc_col = jnp.sum(jnp.where(diagonal, doc_row, 0.0), axis=1, keepdims=True)
    kx[0:TOK, LAT:LAT + ROPE] = dot(diagonal.astype(jnp.bfloat16), kr_v[...], NT).astype(jnp.bfloat16)
    kx[0:TOK, LAT + ROPE:EXT] = jnp.where(
        iota((TOK, ROPE), 1) == 0, doc_col, 0.0
    ).astype(jnp.bfloat16)

    pl.semaphore_wait(barrier, len(partners))

    def tell(sem, *others):
        for other in others:
            pl.semaphore_signal(sem, inc=1, device_id=device(**other), device_id_type=MESH)

    half_rows = TOK // 2

    def half(d):
        return kx.at[pl.ds(pl.multiple_of(d * TOK + c * half_rows, half_rows), half_rows)]

    quarter_rows = TOK // 4

    def quarter(d, n):
        start = pl.multiple_of(d * TOK + c * half_rows + n * quarter_rows, quarter_rows)
        return kx.at[pl.ds(start, quarter_rows)]

    def hz(n):
        return remote(quarter(0, n), quarter(4, n), hz_s.at[n], hz_r.at[n], device(dz=1))

    def hy(j, src, n):
        return remote(
            quarter(src, n), quarter(j, n), hy_s.at[j - 1, n], hy_r.at[j - 1, n], device(dy=j)
        )

    @pl.when(jnp.logical_not(last))
    def _():
        for n in (0, 1):
            hz(n).start()

    for n in (0, 1):
        for j in (3, 1):
            @pl.when(y + j < 4)
            def _():
                hy(j, 0, n).start()

    tell(met, *near)

    def hc(d):
        return remote(half(d), half(d), hc_s.at[d - 1], hc_r.at[d - 1], device(dc=1))

    for n in (0, 1):
        if n == 0:
            pl.semaphore_wait(met, len(near))

        @pl.when(y < 2)
        def _():
            hy(2, 0, n).start()

        @pl.when(jnp.logical_not(first))
        def _():
            hz(n).wait_recv()
            for j in (2, 1, 3):
                @pl.when(y + j >= 4)
                def _():
                    hy(j, 4, n).start()

    for d in (1, 2, 3, 4):
        @pl.when(first & (y < d))
        def _():
            half(d)[...] = jnp.full((half_rows, EXT), -1.0, jnp.bfloat16)

    hc(4).start()
    tell(met_2, dict(dy=2), dict(dx=2), dict(dz=2), dict(dz=14))

    own_head = iota((TILE, LAT), 1) // ROPE == lax.rem(iota((TILE, LAT), 0), HEADS)
    prepare(qx, g, qxt, gt, kx, s_all, gp_all, docq, qr_v, doc_col, own_head, loads)

    for j in (3, 1, 2):
        @pl.when(jnp.logical_not(first & (y < j)))
        def _():
            hy(j, 0, 0).wait_recv()
            hy(j, 0, 1).wait_recv()

        hc(j).start()
    hc(3).wait_recv()
    hc(4).wait_recv()
    products(qx, g, kx, s_all, gp_all, slice(3 * TOK, 5 * TOK))
    pl.semaphore_wait(met_2, 4)
    tell(met_4, dict(dz=4), dict(dz=12))
    hc(1).wait_recv()
    hc(2).wait_recv()
    pick = (iota((8, 128), 1) == ROPE).astype(jnp.bfloat16)
    docs = [dot(pick, kx[d * TOK:(d + 1) * TOK, LAT:EXT], NT)[0:1] for d in range(BLOCKS)]
    beside = [(f, group) for group in GROUPS for f in range(0, EXT, 128)]
    products(qx, g, kx, s_all, gp_all, slice(TOK, 3 * TOK), [0])
    for r in range(0, ROWS, CHUNK):
        if r % TILE == 0 and r + TILE < ROWS:
            products(qx, g, kx, s_all, gp_all, slice(TOK, 3 * TOK), [r + TILE])
        scores(r, docs, s_all, gp_all, docq, p_all, gs_all)
        if r >= ROWS // 2:
            for f, group in beside[:2]:
                cols = slice(group[0] * TOK, (group[-1] + 1) * TOK)
                acc[f:f + 128, cols] = key_sum(
                    qxt, gt, gs_all, p_all, f, group, slice(0, ROWS // 2)
                )
            beside = beside[2:]

    def by_core(step):
        for own in (0, 1):
            pl.when(c == own)(functools.partial(step, own))

    def core_sum(d, giver):
        other = 1 - giver
        return remote(
            part.at[d, pl.ds(START[other], SPAN[other])], part_in.at[d, pl.ds(0, SPAN[other])],
            cs_s.at[d], cs_r.at[d], device(dc=1),
        )

    def piece(own, place):
        return pl.ds(pl.multiple_of(place * PIECE[own], PIECE[own]), PIECE[own])

    def xy(d, i, own):
        to = device(dx=i) if d in (0, 4) else device(dx=i, dy=4 - d)
        return remote(
            summed.at[d, piece(own, lax.rem(x + i, 4))], pieces_in.at[d, i, pl.ds(0, PIECE[own])],
            xy_s.at[d, i], xy_r.at[d, i], to,
        )

    def remote_pieces(d):
        return [i for i in (2, 1, 3, 0) if d not in (0, 4) or i]

    def pass_on(group, own):
        for d in group:
            core_sum(d, 1 - own).wait_recv()
            summed[d, 0:SPAN[own]] = (
                part[d, START[own]:START[own] + SPAN[own]].astype(jnp.float32)
                + part_in[d, 0:SPAN[own]].astype(jnp.float32)
            ).astype(jnp.bfloat16)
            for i in remote_pieces(d):
                xy(d, i, own).start()

    def exchange(group, own):
        for d in group:
            core_sum(d, own).start()

    for n, group in enumerate(GROUPS):
        key_grads(qxt, gt, gs_all, p_all, acc, part, group)
        by_core(functools.partial(exchange, group))
        if n:
            by_core(functools.partial(pass_on, GROUPS[n - 1]))

    outputs(p_all, gs_all, kx, own_head, o_v, dq_v, dqr_v, 0)
    by_core(functools.partial(pass_on, GROUPS[-1]))
    for r in range(TILE, ROWS, TILE):
        outputs(p_all, gs_all, kx, own_head, o_v, dq_v, dqr_v, r)

    def far_copies(own):
        rows = pl.ds(0, PIECE[own])
        return (
            remote(b_out.at[rows], b_in.at[0, rows], zb_s.at[0], zb_r.at[0], device(dz=15)),
            remote(b_out.at[rows], b_in.at[1, rows], zb_s.at[1], zb_r.at[1], device(dz=7)),
            remote(a_out.at[rows], a_in.at[rows], zh_s, zh_r, device(dz=8)),
        )

    def ag(i, other, giver):
        rows = pl.ds(pl.multiple_of(START[giver] + x * PIECE[giver], 16), PIECE[giver])
        return remote(
            total.at[rows], total.at[rows], ag_s.at[i, other], ag_r.at[i, other],
            device(dx=i, dc=other),
        )

    spread = [(i, other) for i in (2, 1, 3, 0) for other in (1, 0) if i or other]

    def finish(own):
        rows = PIECE[own]

        def gathered(d):
            terms = []
            if d in (0, 4):
                terms.append(summed[d, piece(own, x)].astype(jnp.float32))
            for i in remote_pieces(d):
                xy(d, i, own).wait_recv()
                terms.append(pieces_in[d, i, 0:rows].astype(jnp.float32))
            return functools.reduce(jnp.add, terms)

        b = jnp.zeros((rows, TOK), jnp.float32)
        a = jnp.zeros((rows, TOK), jnp.float32)
        for d in (1, 2, 3):
            term = gathered(d)
            same = y + d < 4
            a = a + jnp.where(same, term, 0.0)
            b = b + jnp.where(same, 0.0, term)
        b = b + gathered(4)
        b_out[0:rows] = b.astype(jnp.bfloat16)
        pl.semaphore_wait(met_4, 2)
        near_b, far_b, far_a = far_copies(own)

        @pl.when(jnp.logical_not(first))
        def _():
            far_b.start()

        a = a + gathered(0)
        a_out[0:rows] = a.astype(jnp.bfloat16)
        far_a.start()

        @pl.when(jnp.logical_not(first))
        def _():
            near_b.start()

        @pl.when(last)
        def _():
            b_in[...] = jnp.zeros_like(b_in)

        @pl.when(jnp.logical_not(last))
        def _():
            near_b.wait_recv()
            far_b.wait_recv()

        far_a.wait_recv()
        mine = pl.ds(pl.multiple_of(START[own] + x * rows, 16), rows)
        total[mine, :] = (
            (a_out[0:rows].astype(jnp.float32) + a_in[0:rows].astype(jnp.float32))
            + (b_in[0, 0:rows].astype(jnp.float32) + b_in[1, 0:rows].astype(jnp.float32))
        ).astype(jnp.bfloat16)
        for i, other in spread:
            ag(i, other, own).start()
        for i, other in spread:
            ag(i, other, (own + other) % 2).wait_recv()

    by_core(finish)
    latent_rows = [total[to:to + rows, :] for start, rows, to in PLACES if start < LAT]
    rope_rows = [total[to:to + rows, :] for start, rows, to in PLACES if start >= LAT]
    gl_v[...] = dot(diagonal.astype(jnp.bfloat16), jnp.concatenate(latent_rows, axis=0), NT)
    gk_v[...] = jnp.concatenate(rope_rows, axis=0).astype(jnp.float32)

    for n in (0, 1):
        @pl.when(jnp.logical_not(last))
        def _():
            hz(n).wait_send()

        for j in (1, 2, 3):
            @pl.when(jnp.logical_not(first & (y + j >= 4)))
            def _():
                hy(j, 0, n).wait_send()
    for d in (1, 2, 3, 4):
        hc(d).wait_send()

    def sent(own):
        for d in range(BLOCKS):
            core_sum(d, own).wait_send()
            for i in remote_pieces(d):
                xy(d, i, own).wait_send()
        near_b, far_b, far_a = far_copies(own)

        @pl.when(jnp.logical_not(first))
        def _():
            near_b.wait_send()
            far_b.wait_send()

        far_a.wait_send()
        for i, other in spread:
            ag(i, other, own).wait_send()

    by_core(sent)


def store(*refs):
    sources, targets, sem = refs[:5], refs[5:10], refs[10]
    copies = [pltpu.make_async_copy(sources[n], targets[n], sem.at[n]) for n in range(5)]
    for copy in copies:
        copy.start()
    for copy in copies:
        copy.wait()


def per_device(query_latent, query_rope, latent, key_rope, doc_ids, grad_out):
    bf16, f32 = jnp.bfloat16, jnp.float32
    dma = pltpu.SemaphoreType.DMA
    results = pl.pallas_call(
        kernel,
        out_shape=(
            jax.ShapeDtypeStruct((ROWS, LAT), bf16),
            jax.ShapeDtypeStruct((ROWS, LAT), bf16),
            jax.ShapeDtypeStruct((TOK, LAT), bf16),
            jax.ShapeDtypeStruct((TOK, LAT), f32),
            jax.ShapeDtypeStruct((ROPE, TOK), f32),
        ),
        in_specs=[pl.BlockSpec(memory_space=pltpu.HBM)] * 6,
        out_specs=[pl.BlockSpec(memory_space=pltpu.VMEM)] * 5,
        scratch_shapes=[
            pltpu.VMEM((ROWS, EXT), bf16),
            pltpu.VMEM((ROWS, LAT), bf16),
            pltpu.VMEM((EXT, ROWS), bf16),
            pltpu.VMEM((LAT, ROWS), bf16),
            pltpu.VMEM((KEYS, EXT), bf16),
            pltpu.VMEM((ROWS, KEYS), f32),
            pltpu.VMEM((ROWS, KEYS), f32),
            pltpu.VMEM((ROWS, TOK), f32),
            pltpu.VMEM((ROWS, KEYS), bf16),
            pltpu.VMEM((ROWS, KEYS), bf16),
            pltpu.VMEM((EXT, KEYS), f32),
            pltpu.VMEM((TOK, LAT), bf16),
            pltpu.VMEM((ROPE, TOK), bf16),
            pltpu.VMEM((1, TOK), jnp.int32),
            pltpu.VMEM((BLOCKS, FEATURES, TOK), bf16),
            pltpu.VMEM((BLOCKS, SPAN[0], TOK), bf16),
            pltpu.VMEM((BLOCKS, SPAN[0], TOK), bf16),
            pltpu.VMEM((BLOCKS, 4, PIECE[0], TOK), bf16),
            pltpu.VMEM((PIECE[0], TOK), bf16),
            pltpu.VMEM((2, PIECE[0], TOK), bf16),
            pltpu.VMEM((PIECE[0], TOK), bf16),
            pltpu.VMEM((PIECE[0], TOK), bf16),
            pltpu.VMEM((FEATURES, TOK), bf16),
            dma((6,)),
            dma((2,)), dma((2,)), dma((3, 2)), dma((3, 2)), dma((4,)), dma((4,)),
            dma((BLOCKS,)), dma((BLOCKS,)), dma((BLOCKS, 4)), dma((BLOCKS, 4)),
            dma((2,)), dma((2,)), dma, dma, dma((4, 2)), dma((4, 2)),
            pltpu.SemaphoreType.REGULAR, pltpu.SemaphoreType.REGULAR, pltpu.SemaphoreType.REGULAR,
        ],
        compiler_params=pltpu.CompilerParams(
            collective_id=0, has_side_effects=True, vmem_limit_bytes=48 * 1024 * 1024
        ),
        cost_estimate=pl.CostEstimate(
            flops=9 * 2 * ROWS * KEYS * LAT // 2, bytes_accessed=5 * 1024 * 1024,
            transcendentals=ROWS * KEYS,
        ),
    )(*[
        pltpu.with_memory_space_constraint(array, pltpu.HBM)
        for array in (
            query_latent.reshape(ROWS, LAT), query_rope, latent, key_rope.T,
            doc_ids.reshape(1, TOK), grad_out.reshape(ROWS, LAT),
        )
    ])
    attended, grad_query, grad_query_rope, grad_latent, grad_key_rope = pl.pallas_call(
        store,
        out_shape=tuple(jax.ShapeDtypeStruct(r.shape, r.dtype) for r in results),
        in_specs=[pl.BlockSpec(memory_space=pltpu.VMEM)] * 5,
        out_specs=[pl.BlockSpec(memory_space=pltpu.HBM)] * 5,
        scratch_shapes=[dma((5,))],
        compiler_params=pltpu.CompilerParams(vmem_limit_bytes=4 * 1024 * 1024),
    )(*results)
    return (
        attended.reshape(TOK, HEADS, LAT),
        grad_query.reshape(TOK, HEADS, LAT),
        grad_query_rope,
        grad_latent,
        grad_key_rope.T,
    )


def solution(mesh):
    in_specs = (
        P("ctx", "head", None),
        P("ctx", "head"),
        P("ctx", None),
        P("ctx", None),
        P("ctx"),
        P("ctx", "head", None),
    )
    out_specs = (
        P("ctx", "head", None),
        P("ctx", "head", None),
        P("ctx", "head"),
        P("ctx", None),
        P("ctx", None),
    )
    return jax.shard_map(
        per_device, mesh=mesh, in_specs=in_specs, out_specs=out_specs, check_vma=False
    )
```

```python
import functools

import jax
import jax.numpy as jnp
from jax import lax
from jax.experimental import pallas as pl
from jax.experimental.pallas import tpu as pltpu
from jax.sharding import PartitionSpec as P

SCORE_SCALE = 192.0 ** (-0.5)
LOG2E = 1.4426950408889634
NEGATIVE = -1e30
MESH = pl.DeviceIdType.MESH

TOK = 128
HEADS = 8
ROWS = TOK * HEADS
LAT = 512
ROPE = 64
EXT = 640
BLOCKS = 5
KEYS = TOK * BLOCKS
FEATURES = LAT + ROPE
START = (0, 320)
SPAN = (320, 256)
PIECE = (80, 64)
PLACES = [(64 * n, 64, 80 * n) for n in range(4)] + [(256, 128, 320), (384, 128, 448)]
PLACES += [(LAT + 16 * n, 16, 80 * n + 64) for n in range(4)]
NT = (((1,), (1,)), ((), ()))
NN = (((1,), (0,)), ((), ()))
TILE = 256
CHUNK = 64


def dot(a, b, dims=NN):
    return lax.dot_general(a, b, dims, preferred_element_type=jnp.float32)


def iota(shape, dim):
    return lax.broadcasted_iota(jnp.int32, shape, dim)


def products(qx, g, kx, s_all, gp_all, keys, tiles=range(0, ROWS, TILE)):
    for r in tiles:
        s_all[r:r + TILE, keys] = dot(qx[r:r + TILE, :], kx[keys, :], NT)
        gp_all[r:r + TILE, keys] = dot(g[r:r + TILE, :], kx[keys, 0:LAT], NT)


def prepare(qx, g, qxt, gt, kx, s_all, gp_all, docq, qr_v, doc_col, own_head, loads):
    docq[...] = dot(
        (iota((ROWS, TOK), 0) // HEADS == iota((ROWS, TOK), 1)).astype(jnp.bfloat16),
        jnp.broadcast_to(doc_col, (TOK, TOK)).astype(jnp.bfloat16),
    )
    loads[3].wait()
    for r in range(0, ROWS, TILE):
        spread = (r // HEADS + iota((TILE, TOK), 0) // HEADS == iota((TILE, TOK), 1)).astype(jnp.bfloat16)
        wide = jnp.where(own_head, dot(spread, qr_v[...]), 0.0)
        pair = (wide[:, 0:128] + wide[:, 128:256]) + (wide[:, 256:384] + wide[:, 384:512])
        low = jnp.where(iota((TILE, 128), 1) < ROPE, pair + pltpu.roll(pair, ROPE, 1), 0.0)
        qx[r:r + TILE, LAT:EXT] = low.astype(jnp.bfloat16)
    loads[4].wait()
    loads[5].wait()
    products(qx, g, kx, s_all, gp_all, slice(0, TOK))
    for r in range(0, ROWS, TILE):
        qxt[:, r:r + TILE] = qx[r:r + TILE, :].T
        gt[:, r:r + TILE] = g[r:r + TILE, :].T


def scores(r, docs, s_all, gp_all, docq, p_all, gs_all):
    rows = slice(r, r + CHUNK)
    doc_here = docq[rows, :]
    causal = r // HEADS + iota((CHUNK, TOK), 0) // HEADS >= iota((CHUNK, TOK), 1)

    def tile(ref, d):
        return ref[rows, d * TOK:(d + 1) * TOK]

    docs = [jnp.where(causal, docs[0], docs[4])] + docs[1:4]
    score = [jnp.where(causal, tile(s_all, 0), tile(s_all, 4))] + [tile(s_all, d) for d in (1, 2, 3)]
    gp = [jnp.where(causal, tile(gp_all, 0), tile(gp_all, 4))] + [tile(gp_all, d) for d in (1, 2, 3)]
    score = [jnp.where(doc_here == docs[n], score[n], NEGATIVE) for n in range(4)]
    most = functools.reduce(jnp.maximum, score)
    most = jnp.max(most, axis=1, keepdims=True) * (SCORE_SCALE * LOG2E)
    weight = [jnp.exp2(part * (SCORE_SCALE * LOG2E) - most) for part in score]
    norm = jnp.sum(functools.reduce(jnp.add, weight), axis=1, keepdims=True)
    delta = functools.reduce(jnp.add, [w * t for w, t in zip(weight, gp)])
    delta = jnp.sum(delta, axis=1, keepdims=True)
    inverse = 1.0 / norm
    delta = delta * inverse
    for n in range(4):
        prob = weight[n] * inverse
        grad = (SCORE_SCALE * prob) * (gp[n] - delta)
        for ref, value in ((p_all, prob), (gs_all, grad)):
            if n:
                ref[rows, n * TOK:(n + 1) * TOK] = value.astype(jnp.bfloat16)
            else:
                ref[rows, 0:TOK] = jnp.where(causal, value, 0.0).astype(jnp.bfloat16)
                ref[rows, 4 * TOK:5 * TOK] = jnp.where(causal, 0.0, value).astype(jnp.bfloat16)


GROUPS = ((1, 2), (3, 4), (0,))


def key_sum(qxt, gt, gs_all, p_all, f, group, rows):
    cols = slice(group[0] * TOK, (group[-1] + 1) * TOK)
    grads = dot(qxt[f:f + 128, rows], gs_all[rows, cols])
    if f < LAT:
        grads = grads + dot(gt[f:f + 128, rows], p_all[rows, cols])
    return grads


def key_grads(qxt, gt, gs_all, p_all, acc, part, group):
    for f in range(0, EXT, 128):
        grads = key_sum(qxt, gt, gs_all, p_all, f, group, slice(ROWS // 2, ROWS))
        for k, d in enumerate(group):
            block = (
                grads[:, k * TOK:(k + 1) * TOK] + acc[f:f + 128, d * TOK:(d + 1) * TOK]
            ).astype(jnp.bfloat16)
            for start, rows, to in PLACES:
                if f <= start < f + 128:
                    part[d, to:to + rows, :] = block[start - f:start - f + rows]


def outputs(p_all, gs_all, kx, own_head, o_v, dq_v, dqr_v, r):
    o_v[r:r + TILE, :] = dot(p_all[r:r + TILE, :], kx[:, 0:LAT]).astype(jnp.bfloat16)
    grads = dot(gs_all[r:r + TILE, :], kx[...])
    dq_v[r:r + TILE, :] = grads[:, 0:LAT].astype(jnp.bfloat16)
    low = jnp.where(iota((TILE, 128), 1) < ROPE, grads[:, LAT:EXT], 0.0)
    pair = low + pltpu.roll(low, ROPE, 1)
    wide = jnp.where(own_head, jnp.concatenate([pair] * 4, axis=1), 0.0).astype(jnp.bfloat16)
    tokens = TILE // HEADS
    gather = (iota((tokens, TILE), 1) // HEADS == iota((tokens, TILE), 0)).astype(jnp.bfloat16)
    dqr_v[r // HEADS:r // HEADS + tokens, :] = dot(gather, wide).astype(jnp.bfloat16)


def kernel(
    ql, qr, lat, kr, doc, go,
    o_v, dq_v, dqr_v, gl_v, gk_v,
    qx, g, qxt, gt, kx, s_all, gp_all, docq, p_all, gs_all, acc,
    qr_v, kr_v, doc_v,
    part, part_in, summed, pieces_in, b_out, b_in, a_out, a_in, total,
    in_sem, hz_s, hz_r, hy_s, hy_r, hc_s, hc_r,
    cs_s, cs_r, xy_s, xy_r, zb_s, zb_r, zh_s, zh_r, ag_s, ag_r, met, met_2, met_4,
):
    ctx = lax.axis_index("ctx")
    head = lax.axis_index("head")
    z = lax.rem(head // 8 * 8 + ctx // 4, 16)
    y = lax.rem(ctx, 4)
    x = lax.rem(head // 2, 4)
    c = lax.rem(head, 2)
    first = ctx < 4
    last = ctx >= 28

    def device(dz=0, dy=0, dx=0, dc=0):
        zz = lax.rem(z + dz, 16)
        yy = lax.rem(y + dy, 4)
        xx = lax.rem(x + dx, 4)
        cc = lax.rem(c + dc, 2)
        return (lax.rem(zz, 8) * 4 + yy, zz // 8 * 8 + xx * 2 + cc)

    def remote(src, dst, send, recv, to):
        return pltpu.make_async_remote_copy(
            src_ref=src, dst_ref=dst, send_sem=send, recv_sem=recv,
            device_id=to, device_id_type=MESH,
        )

    near = [dict(dy=1), dict(dy=3), dict(dz=1), dict(dz=15), dict(dx=1), dict(dx=3)]
    partners = near + [dict(dc=1)]
    barrier = pltpu.get_barrier_semaphore()
    for partner in partners:
        pl.semaphore_signal(barrier, inc=1, device_id=device(**partner), device_id_type=MESH)

    loads = [
        pltpu.make_async_copy(src, dst, in_sem.at[n])
        for n, (src, dst) in enumerate([
            (lat, kx.at[pl.ds(0, TOK), pl.ds(0, LAT)]), (kr, kr_v), (doc, doc_v), (qr, qr_v),
            (ql, qx.at[:, pl.ds(0, LAT)]), (go, g),
        ])
    ]
    for load in loads:
        load.start()

    for load in loads[:3]:
        load.wait()
    doc_row = jnp.broadcast_to(doc_v[...].astype(jnp.float32), (TOK, TOK))
    diagonal = iota((TOK, TOK), 0) == iota((TOK, TOK), 1)
    doc_col = jnp.sum(jnp.where(diagonal, doc_row, 0.0), axis=1, keepdims=True)
    kx[0:TOK, LAT:LAT + ROPE] = dot(diagonal.astype(jnp.bfloat16), kr_v[...], NT).astype(jnp.bfloat16)
    kx[0:TOK, LAT + ROPE:EXT] = jnp.where(
        iota((TOK, ROPE), 1) == 0, doc_col, 0.0
    ).astype(jnp.bfloat16)

    pl.semaphore_wait(barrier, len(partners))

    def tell(sem, *others):
        for other in others:
            pl.semaphore_signal(sem, inc=1, device_id=device(**other), device_id_type=MESH)

    half_rows = TOK // 2

    def half(d):
        return kx.at[pl.ds(pl.multiple_of(d * TOK + c * half_rows, half_rows), half_rows)]

    quarter_rows = TOK // 4

    def quarter(d, n):
        start = pl.multiple_of(d * TOK + c * half_rows + n * quarter_rows, quarter_rows)
        return kx.at[pl.ds(start, quarter_rows)]

    def hz(n):
        return remote(quarter(0, n), quarter(4, n), hz_s.at[n], hz_r.at[n], device(dz=1))

    def hy(j, src, n):
        return remote(
            quarter(src, n), quarter(j, n), hy_s.at[j - 1, n], hy_r.at[j - 1, n], device(dy=j)
        )

    @pl.when(jnp.logical_not(last))
    def _():
        for n in (0, 1):
            hz(n).start()

    for n in (0, 1):
        for j in (3, 1):
            @pl.when(y + j < 4)
            def _():
                hy(j, 0, n).start()

    tell(met, *near)

    def hc(d):
        return remote(half(d), half(d), hc_s.at[d - 1], hc_r.at[d - 1], device(dc=1))

    for n in (0, 1):
        if n == 0:
            pl.semaphore_wait(met, len(near))

        @pl.when(y < 2)
        def _():
            hy(2, 0, n).start()

        @pl.when(jnp.logical_not(first))
        def _():
            hz(n).wait_recv()
            for j in (2, 1, 3):
                @pl.when(y + j >= 4)
                def _():
                    hy(j, 4, n).start()

    for d in (1, 2, 3, 4):
        @pl.when(first & (y < d))
        def _():
            half(d)[...] = jnp.full((half_rows, EXT), -1.0, jnp.bfloat16)

    hc(4).start()
    tell(met_2, dict(dy=2), dict(dx=2), dict(dz=2), dict(dz=14))

    own_head = iota((TILE, LAT), 1) // ROPE == lax.rem(iota((TILE, LAT), 0), HEADS)
    prepare(qx, g, qxt, gt, kx, s_all, gp_all, docq, qr_v, doc_col, own_head, loads)

    for j in (3, 1, 2):
        @pl.when(jnp.logical_not(first & (y < j)))
        def _():
            hy(j, 0, 0).wait_recv()
            hy(j, 0, 1).wait_recv()

        hc(j).start()
    hc(3).wait_recv()
    hc(4).wait_recv()
    products(qx, g, kx, s_all, gp_all, slice(3 * TOK, 5 * TOK))
    pl.semaphore_wait(met_2, 4)
    tell(met_4, dict(dz=4), dict(dz=12))
    hc(1).wait_recv()
    hc(2).wait_recv()
    pick = (iota((8, 128), 1) == ROPE).astype(jnp.bfloat16)
    docs = [dot(pick, kx[d * TOK:(d + 1) * TOK, LAT:EXT], NT)[0:1] for d in range(BLOCKS)]
    beside = [(f, group) for group in GROUPS for f in range(0, EXT, 128)]
    products(qx, g, kx, s_all, gp_all, slice(TOK, 3 * TOK), [0])
    for r in range(0, ROWS, CHUNK):
        if r % TILE == 0 and r + TILE < ROWS:
            products(qx, g, kx, s_all, gp_all, slice(TOK, 3 * TOK), [r + TILE])
        scores(r, docs, s_all, gp_all, docq, p_all, gs_all)
        if r >= ROWS // 2:
            for f, group in beside[:2]:
                cols = slice(group[0] * TOK, (group[-1] + 1) * TOK)
                acc[f:f + 128, cols] = key_sum(
                    qxt, gt, gs_all, p_all, f, group, slice(0, ROWS // 2)
                )
            beside = beside[2:]

    def by_core(step):
        for own in (0, 1):
            pl.when(c == own)(functools.partial(step, own))

    def core_sum(d, giver):
        other = 1 - giver
        return remote(
            part.at[d, pl.ds(START[other], SPAN[other])], part_in.at[d, pl.ds(0, SPAN[other])],
            cs_s.at[d], cs_r.at[d], device(dc=1),
        )

    def piece(own, place):
        return pl.ds(pl.multiple_of(place * PIECE[own], PIECE[own]), PIECE[own])

    def xy(d, i, own):
        to = device(dx=i) if d in (0, 4) else device(dx=i, dy=4 - d)
        return remote(
            summed.at[d, piece(own, lax.rem(x + i, 4))], pieces_in.at[d, i, pl.ds(0, PIECE[own])],
            xy_s.at[d, i], xy_r.at[d, i], to,
        )

    def remote_pieces(d):
        return [i for i in (2, 1, 3, 0) if d not in (0, 4) or i]

    def pass_on(group, own):
        for d in group:
            core_sum(d, 1 - own).wait_recv()
            summed[d, 0:SPAN[own]] = (
                part[d, START[own]:START[own] + SPAN[own]].astype(jnp.float32)
                + part_in[d, 0:SPAN[own]].astype(jnp.float32)
            ).astype(jnp.bfloat16)
            for i in remote_pieces(d):
                xy(d, i, own).start()

    def exchange(group, own):
        for d in group:
            core_sum(d, own).start()

    for n, group in enumerate(GROUPS):
        key_grads(qxt, gt, gs_all, p_all, acc, part, group)
        by_core(functools.partial(exchange, group))
        if n:
            by_core(functools.partial(pass_on, GROUPS[n - 1]))

    outputs(p_all, gs_all, kx, own_head, o_v, dq_v, dqr_v, 0)
    by_core(functools.partial(pass_on, GROUPS[-1]))
    for r in range(TILE, ROWS, TILE):
        outputs(p_all, gs_all, kx, own_head, o_v, dq_v, dqr_v, r)

    def far_copies(own):
        rows = pl.ds(0, PIECE[own])
        return (
            remote(b_out.at[rows], b_in.at[0, rows], zb_s.at[0], zb_r.at[0], device(dz=15)),
            remote(b_out.at[rows], b_in.at[1, rows], zb_s.at[1], zb_r.at[1], device(dz=7)),
            remote(a_out.at[rows], a_in.at[rows], zh_s, zh_r, device(dz=8)),
        )

    def ag(i, other, giver):
        rows = pl.ds(pl.multiple_of(START[giver] + x * PIECE[giver], 16), PIECE[giver])
        return remote(
            total.at[rows], total.at[rows], ag_s.at[i, other], ag_r.at[i, other],
            device(dx=i, dc=other),
        )

    spread = [(i, other) for i in (2, 1, 3, 0) for other in (1, 0) if i or other]

    def finish(own):
        rows = PIECE[own]

        def gathered(d):
            terms = []
            if d in (0, 4):
                terms.append(summed[d, piece(own, x)].astype(jnp.float32))
            for i in remote_pieces(d):
                xy(d, i, own).wait_recv()
                terms.append(pieces_in[d, i, 0:rows].astype(jnp.float32))
            return functools.reduce(jnp.add, terms)

        b = jnp.zeros((rows, TOK), jnp.float32)
        a = jnp.zeros((rows, TOK), jnp.float32)
        for d in (1, 2, 3):
            term = gathered(d)
            same = y + d < 4
            a = a + jnp.where(same, term, 0.0)
            b = b + jnp.where(same, 0.0, term)
        b = b + gathered(4)
        b_out[0:rows] = b.astype(jnp.bfloat16)
        pl.semaphore_wait(met_4, 2)
        near_b, far_b, far_a = far_copies(own)

        @pl.when(jnp.logical_not(first))
        def _():
            far_b.start()

        a = a + gathered(0)
        a_out[0:rows] = a.astype(jnp.bfloat16)
        far_a.start()

        @pl.when(jnp.logical_not(first))
        def _():
            near_b.start()

        @pl.when(last)
        def _():
            b_in[...] = jnp.zeros_like(b_in)

        @pl.when(jnp.logical_not(last))
        def _():
            near_b.wait_recv()
            far_b.wait_recv()

        far_a.wait_recv()
        mine = pl.ds(pl.multiple_of(START[own] + x * rows, 16), rows)
        total[mine, :] = (
            (a_out[0:rows].astype(jnp.float32) + a_in[0:rows].astype(jnp.float32))
            + (b_in[0, 0:rows].astype(jnp.float32) + b_in[1, 0:rows].astype(jnp.float32))
        ).astype(jnp.bfloat16)
        for i, other in spread:
            ag(i, other, own).start()
        for i, other in spread:
            ag(i, other, (own + other) % 2).wait_recv()

    by_core(finish)
    latent_rows = [total[to:to + rows, :] for start, rows, to in PLACES if start < LAT]
    rope_rows = [total[to:to + rows, :] for start, rows, to in PLACES if start >= LAT]
    gl_v[...] = dot(diagonal.astype(jnp.bfloat16), jnp.concatenate(latent_rows, axis=0), NT)
    gk_v[...] = jnp.concatenate(rope_rows, axis=0).astype(jnp.float32)

    for n in (0, 1):
        @pl.when(jnp.logical_not(last))
        def _():
            hz(n).wait_send()

        for j in (1, 2, 3):
            @pl.when(jnp.logical_not(first & (y + j >= 4)))
            def _():
                hy(j, 0, n).wait_send()
    for d in (1, 2, 3, 4):
        hc(d).wait_send()

    def sent(own):
        for d in range(BLOCKS):
            core_sum(d, own).wait_send()
            for i in remote_pieces(d):
                xy(d, i, own).wait_send()
        near_b, far_b, far_a = far_copies(own)

        @pl.when(jnp.logical_not(first))
        def _():
            near_b.wait_send()
            far_b.wait_send()

        far_a.wait_send()
        for i, other in spread:
            ag(i, other, own).wait_send()

    by_core(sent)


def store(*refs):
    sources, targets, sem = refs[:5], refs[5:10], refs[10]
    copies = [pltpu.make_async_copy(sources[n], targets[n], sem.at[n]) for n in range(5)]
    for copy in copies:
        copy.start()
    for copy in copies:
        copy.wait()


def per_device(query_latent, query_rope, latent, key_rope, doc_ids, grad_out):
    bf16, f32 = jnp.bfloat16, jnp.float32
    dma = pltpu.SemaphoreType.DMA
    results = pl.pallas_call(
        kernel,
        out_shape=(
            jax.ShapeDtypeStruct((ROWS, LAT), bf16),
            jax.ShapeDtypeStruct((ROWS, LAT), bf16),
            jax.ShapeDtypeStruct((TOK, LAT), bf16),
            jax.ShapeDtypeStruct((TOK, LAT), f32),
            jax.ShapeDtypeStruct((ROPE, TOK), f32),
        ),
        in_specs=[pl.BlockSpec(memory_space=pltpu.HBM)] * 6,
        out_specs=[pl.BlockSpec(memory_space=pltpu.VMEM)] * 5,
        scratch_shapes=[
            pltpu.VMEM((ROWS, EXT), bf16),
            pltpu.VMEM((ROWS, LAT), bf16),
            pltpu.VMEM((EXT, ROWS), bf16),
            pltpu.VMEM((LAT, ROWS), bf16),
            pltpu.VMEM((KEYS, EXT), bf16),
            pltpu.VMEM((ROWS, KEYS), f32),
            pltpu.VMEM((ROWS, KEYS), f32),
            pltpu.VMEM((ROWS, TOK), f32),
            pltpu.VMEM((ROWS, KEYS), bf16),
            pltpu.VMEM((ROWS, KEYS), bf16),
            pltpu.VMEM((EXT, KEYS), f32),
            pltpu.VMEM((TOK, LAT), bf16),
            pltpu.VMEM((ROPE, TOK), bf16),
            pltpu.VMEM((1, TOK), jnp.int32),
            pltpu.VMEM((BLOCKS, FEATURES, TOK), bf16),
            pltpu.VMEM((BLOCKS, SPAN[0], TOK), bf16),
            pltpu.VMEM((BLOCKS, SPAN[0], TOK), bf16),
            pltpu.VMEM((BLOCKS, 4, PIECE[0], TOK), bf16),
            pltpu.VMEM((PIECE[0], TOK), bf16),
            pltpu.VMEM((2, PIECE[0], TOK), bf16),
            pltpu.VMEM((PIECE[0], TOK), bf16),
            pltpu.VMEM((PIECE[0], TOK), bf16),
            pltpu.VMEM((FEATURES, TOK), bf16),
            dma((6,)),
            dma((2,)), dma((2,)), dma((3, 2)), dma((3, 2)), dma((4,)), dma((4,)),
            dma((BLOCKS,)), dma((BLOCKS,)), dma((BLOCKS, 4)), dma((BLOCKS, 4)),
            dma((2,)), dma((2,)), dma, dma, dma((4, 2)), dma((4, 2)),
            pltpu.SemaphoreType.REGULAR, pltpu.SemaphoreType.REGULAR, pltpu.SemaphoreType.REGULAR,
        ],
        compiler_params=pltpu.CompilerParams(
            collective_id=0, has_side_effects=True, vmem_limit_bytes=48 * 1024 * 1024
        ),
        cost_estimate=pl.CostEstimate(
            flops=9 * 2 * ROWS * KEYS * LAT // 2, bytes_accessed=5 * 1024 * 1024,
            transcendentals=ROWS * KEYS,
        ),
    )(*[
        pltpu.with_memory_space_constraint(array, pltpu.HBM)
        for array in (
            query_latent.reshape(ROWS, LAT), query_rope, latent, key_rope.T,
            doc_ids.reshape(1, TOK), grad_out.reshape(ROWS, LAT),
        )
    ])
    attended, grad_query, grad_query_rope, grad_latent, grad_key_rope = pl.pallas_call(
        store,
        out_shape=tuple(jax.ShapeDtypeStruct(r.shape, r.dtype) for r in results),
        in_specs=[pl.BlockSpec(memory_space=pltpu.VMEM)] * 5,
        out_specs=[pl.BlockSpec(memory_space=pltpu.HBM)] * 5,
        scratch_shapes=[dma((5,))],
        compiler_params=pltpu.CompilerParams(vmem_limit_bytes=4 * 1024 * 1024),
    )(*results)
    return (
        attended.reshape(TOK, HEADS, LAT),
        grad_query.reshape(TOK, HEADS, LAT),
        grad_query_rope,
        grad_latent,
        grad_key_rope.T,
    )


def solution(mesh):
    in_specs = (
        P("ctx", "head", None),
        P("ctx", "head"),
        P("ctx", None),
        P("ctx", None),
        P("ctx"),
        P("ctx", "head", None),
    )
    out_specs = (
        P("ctx", "head", None),
        P("ctx", "head", None),
        P("ctx", "head"),
        P("ctx", None),
        P("ctx", None),
    )
    return jax.shard_map(
        per_device, mesh=mesh, in_specs=in_specs, out_specs=out_specs, check_vma=False
    )
```
